256 devices in a mesh: ia: 4 (over x), ja: 8 (over z_hi, y), ka: 8 (over z_lo, core).
Axes of the slice: x: 4, y: 4, z: 8 (z_hi: 2, z_lo: 4; z = z_hi * 4 + z_lo), core: 2. Of those that a mesh axis runs over, the one named last changes fastest.
Arguments:
- inputs: bfloat16 [4, 2048, 4096], P('ia', 'ja', 'ka'), may hold values from -0.0625 to 0.0625
- attn_out: bfloat16 [4, 2048, 4096], P(None, 'ja', ('ia', 'ka')), may hold values from -0.0625 to 0.0625
- grad_out: bfloat16 [4, 2048, 4096], P('ia', 'ja', 'ka'), may hold values from -6 to 6
- grad_query: bfloat16 [4, 2048, 4096], P(None, 'ja', ('ia', 'ka')), may hold values from -6 to 6
- grad_key: bfloat16 [4, 2048, 4096], P(None, 'ja', ('ia', 'ka')), may hold values from -6 to 6
- grad_value: bfloat16 [4, 2048, 4096], P(None, 'ja', ('ia', 'ka')), may hold values from -6 to 6
- query_weight: bfloat16 [4096, 4096], P('ka', ('ia', 'ja')), may hold values from -0.09375 to 0.09375
- key_weight: bfloat16 [4096, 4096], P('ka', ('ia', 'ja')), may hold values from -0.09375 to 0.09375
- value_weight: bfloat16 [4096, 4096], P('ka', ('ia', 'ja')), may hold values from -0.09375 to 0.09375
Outputs:
- grad_inputs: bfloat16 [4, 2048, 4096], P('ia', 'ja', 'ka')
- query_weight_grad: float32 [4096, 4096], P('ka', ('ia', 'ja'))
- key_weight_grad: float32 [4096, 4096], P('ka', ('ia', 'ja'))
- value_weight_grad: float32 [4096, 4096], P('ka', ('ia', 'ja'))
- output_weight_grad: float32 [4096, 4096], P(('ia', 'ja'), 'ka')
The draws below stay inside these ranges and needn't reach their ends.
All inputs are finite; a program needn't handle non-finite values.
Results may differ from the reference program's by a relative error of at most 0.015.
Values may be sent and summed in bfloat16 or wider, within the bound.
A program may use at most 128 MiB of HBM per device.

```python
import jax
import jax.numpy as jnp

D = 4096
F = 4096
BANKS = 4
BANK_TOK = 2048
TOKENS = 8192


def level_of(key, extent, cuts, low, top_value):
    gain = 1.0
    for position, shards_of in cuts:
        heights = jax.random.uniform(jax.random.fold_in(jax.random.fold_in(key, 6), position), (shards_of,), jnp.float32, low / len(cuts), top_value / len(cuts))
        gain = gain * jnp.repeat(jnp.exp(heights), extent[position] // shards_of).reshape((-1,) + (1,) * (len(extent) - 1 - position))
    return gain


def gaussian(key, dims, deviation, bound, split=(), kind=jnp.bfloat16):
    values = jax.random.normal(key, dims, jnp.float32) * deviation
    if len(split) > 0:
        values = level_of(key, dims, split, -0.22, 0.18) * values
    return jnp.clip(values, min=-bound, max=bound).astype(kind)


def setup_inputs(seed: int = 0) -> dict:
    streams_of = jax.random.split(jax.random.key(seed), 10)
    return {
        "inputs": gaussian(streams_of[0], (BANKS, BANK_TOK, D), (TOKENS ** -0.5), 0.0625, ((0, 4), (1, 8), (2, 8))),
        "attn_out": gaussian(streams_of[1], (BANKS, BANK_TOK, F), (TOKENS ** -0.5), 0.0625, ((1, 8), (2, 32))),
        "grad_out": gaussian(streams_of[2], (BANKS, BANK_TOK, D), 1.0, 6.0, ((0, 4), (1, 8), (2, 8))),
        "grad_query": gaussian(streams_of[3], (BANKS, BANK_TOK, F), 1.0, 6.0, ((1, 8), (2, 32))),
        "grad_key": gaussian(streams_of[4], (BANKS, BANK_TOK, F), 1.0, 6.0, ((1, 8), (2, 32))),
        "grad_value": gaussian(streams_of[5], (BANKS, BANK_TOK, F), 1.0, 6.0, ((1, 8), (2, 32))),
        "query_weight": gaussian(streams_of[6], (D, F), D ** -0.5, 0.09375, ((0, 8), (1, 32))),
        "key_weight": gaussian(streams_of[7], (D, F), D ** -0.5, 0.09375, ((0, 8), (1, 32))),
        "value_weight": gaussian(streams_of[8], (D, F), D ** -0.5, 0.09375, ((0, 8), (1, 32))),
    }


def flatten_rows(array):
    return array.reshape(-1, array.shape[-1])


def reference(inputs, attn_out, grad_out, grad_query, grad_key, grad_value, query_weight, key_weight, value_weight):
    rows_in = flatten_rows(inputs)
    rows_attn = flatten_rows(attn_out)
    rows_grad = flatten_rows(grad_out)
    grad_q = flatten_rows(grad_query)
    grad_k = flatten_rows(grad_key)
    grad_v = flatten_rows(grad_value)
    summed = jnp.dot(grad_q, query_weight.T, preferred_element_type=jnp.float32)
    summed = summed + jnp.dot(grad_k, key_weight.T, preferred_element_type=jnp.float32)
    summed = summed + jnp.dot(grad_v, value_weight.T, preferred_element_type=jnp.float32)
    grad_inputs = summed.astype(jnp.bfloat16).reshape(inputs.shape)
    query_weight_grad = jnp.dot(rows_in.T, grad_q, preferred_element_type=jnp.float32)
    key_weight_grad = jnp.dot(rows_in.T, grad_k, preferred_element_type=jnp.float32)
    value_weight_grad = jnp.dot(rows_in.T, grad_v, preferred_element_type=jnp.float32)
    output_weight_grad = jnp.dot(rows_attn.T, rows_grad, preferred_element_type=jnp.float32)
    return (grad_inputs, query_weight_grad, key_weight_grad, value_weight_grad, output_weight_grad)
```

```python
import functools

import jax
import jax.numpy as jnp
from jax import lax
from jax.experimental import pallas as pl
from jax.experimental.pallas import tpu as pltpu
from jax.sharding import PartitionSpec as P

MESH = pl.DeviceIdType.MESH
BF16 = jnp.bfloat16
F32 = jnp.float32
ATTN = 3


def contract_rows(a, b):
    return lax.dot_general(a, b, (((0,), (0,)), ((), ())), preferred_element_type=F32)


def contract_columns(a, b):
    return lax.dot_general(a, b, (((1,), (1,)), ((), ())), preferred_element_type=F32)


def exchange_kernel(
    in_ref, go_ref, gq_ref, gk_ref, gv_ref, at_ref, wq_ref, wk_ref, wv_ref,
    zr, zro, gz, gown,
    xb, gb, wb, ys, yso, yr, yro, zs, zso, xs, xr, gzs, ownv,
    loc_sem, xz_s, xz_r, xo_s, xo_r, xf_s, xf_r,
    gz_s, gz_r, gc_s, gc_r, gf_s, gf_r,
    wz_s, wz_r, wy_s, wy_r, dy_s, dy_r, dz_s, dz_r,
    gx_s, gx_r, gg_s, gg_r,
):
    ia, ja, ka = lax.axis_index("ia"), lax.axis_index("ja"), lax.axis_index("ka")
    x, y, zh = ia, ja % 4, ja // 4
    zl, c = ka // 2, ka % 2
    zl1, zl0 = zl // 2, zl % 2

    def device(x_=None, y_=None, zh_=None, zl_=None, c_=None):
        x_ = x if x_ is None else x_
        y_ = y if y_ is None else y_
        zh_ = zh if zh_ is None else zh_
        zl_ = zl if zl_ is None else zl_
        c_ = c if c_ is None else c_
        return (x_, zh_ * 4 + y_, zl_ * 2 + c_)

    def flip(bit):
        return 1 - bit

    zl_side = zl1 * 2 + flip(zl0)
    zl_far = flip(zl1) * 2 + zl0
    side, far, core = device(zl_=zl_side), device(zl_=zl_far), device(c_=flip(c))
    over, over_far = device(zh_=flip(zh)), device(zh_=flip(zh), zl_=zl_far)
    x_peer = [device(x_=(x + d) % 4) for d in (1, 2, 3)]
    y_peer = [device(y_=(y + d) % 4) for d in (1, 2, 3)]
    near_first = (0, 2, 1)

    def remote(src, dst, send, recv, to):
        return pltpu.make_async_remote_copy(
            src_ref=src, dst_ref=dst, send_sem=send, recv_sem=recv,
            device_id=to, device_id_type=MESH,
        )

    sent = []

    def start(copy):
        copy.start()
        sent.append(copy)

    def lanes(k):
        return pl.ds(pl.multiple_of(k * 128, 128), 128)

    def bank(b):
        return pl.ds(pl.multiple_of(b * 256, 256), 256)

    g_refs = (gq_ref, gk_ref, gv_ref, at_ref)
    w_refs = (wq_ref, wk_ref, wv_ref)
    x_refs = (in_ref, go_ref)
    k_own, k_side = zl0 * 2 + c, flip(zl0) * 2 + c

    def own_g(a):
        return pltpu.make_async_copy(g_refs[a], gb.at[a, :, lanes(k_own)], loc_sem.at[a])

    def own_x(t):
        return pltpu.make_async_copy(x_refs[t], xb.at[t, zl1, bank(x)], loc_sem.at[4 + t])

    for a in (ATTN, 0, 1, 2):
        own_g(a).start()
    for t in (1, 0):
        own_x(t).start()

    def g_side(a):
        return remote(g_refs[a], gb.at[a, :, lanes(k_own)], gz_s.at[a], gz_r.at[a], side)

    def g_core(a):
        return remote(g_refs[a], gb.at[a, :, lanes(k_own)], gc_s.at[a], gc_r.at[a], core)

    def g_pass(a):
        place = gb.at[a, :, lanes(k_side)]
        return remote(place, place, gf_s.at[a], gf_r.at[a], core)

    def x_far(t):
        return remote(x_refs[t], xb.at[t, zl1, bank(x)], xz_s.at[t], xz_r.at[t], far)

    def x_own(t, d):
        return remote(x_refs[t], xb.at[t, zl1, bank(x)], xo_s.at[t, d], xo_r.at[t, d], x_peer[d])

    def x_pass(t, d):
        place = xb.at[t, flip(zl1), bank(x)]
        return remote(place, place, xf_s.at[t, d], xf_r.at[t, d], x_peer[d])

    w_line = 2 * zh + zl0
    home = zl1 == zh

    def w_place(a, k):
        return wb.at[a, k, :, lanes(y)]

    def w_over(a):
        return remote(w_refs[a], w_place(a, zl1), wz_s.at[a, 0], wz_r.at[a, zl1], device(zh_=flip(zh), zl_=w_line))

    def w_here(a):
        return remote(w_refs[a], w_place(a, zl1), wz_s.at[a, 1], wz_r.at[a, zl1], far)

    def w_self(a):
        return pltpu.make_async_copy(w_refs[a], w_place(a, zl1), wz_r.at[a, zl1])

    def w_arrival(a, k):
        return remote(w_place(a, k), w_place(a, k), wz_s.at[a, 0], wz_r.at[a, k], far)

    def w_pass(a, d):
        place = wb.at[a, :, :, lanes(y)]
        return remote(place, place, wy_s.at[a, d], wy_r.at[a, d], y_peer[d])

    def send_w(a):
        start(w_over(a))

        @pl.when(home)
        def _():
            w_self(a).start()

        @pl.when(jnp.logical_not(home))
        def _():
            w_here(a).start()

    def pass_w(a):
        for k in (0, 1):
            w_arrival(a, k).wait_recv()
        for d in near_first:
            start(w_pass(a, d))

    barrier = pltpu.get_barrier_semaphore()
    peers = x_peer + y_peer + [side, far, core, over, over_far]
    for peer in peers:
        pl.semaphore_signal(barrier, inc=1, device_id=peer, device_id_type=MESH)
    pl.semaphore_wait(barrier, len(peers))

    send_w(0)
    for d in near_first:
        start(x_own(1, d))
    start(g_side(ATTN))
    start(g_core(ATTN))
    start(x_far(1))
    for d in near_first:
        start(x_own(0, d))
    send_w(1)
    start(x_far(0))
    send_w(2)
    for a in (0, 1, 2):
        start(g_side(a))
        start(g_core(a))

    def pass_x(t):
        x_far(t).wait_recv()
        for d in near_first:
            start(x_pass(t, d))

    def pass_g(a):
        g_side(a).wait_recv()
        start(g_pass(a))

    def have_x(t):
        own_x(t).wait()
        for d in (0, 1, 2):
            x_own(t, d).wait_recv()
        for d in (0, 1, 2):
            x_pass(t, d).wait_recv()

    def have_g(a):
        own_g(a).wait()
        g_core(a).wait_recv()
        g_pass(a).wait_recv()

    def y_send(a, d):
        to = (y + d + 1) % 4
        if a == ATTN:
            return remote(yso.at[to], yro.at[d], dy_s.at[a, d], dy_r.at[a, d], y_peer[d])
        return remote(ys.at[a, to], yr.at[a, d], dy_s.at[a, d], dy_r.at[a, d], y_peer[d])

    def output_term():
        @pl.loop(0, 4)
        def _(i):
            k, h = i // 2, i % 2
            part = contract_rows(
                gb[ATTN, :, pl.ds(pl.multiple_of(h * 256, 256), 256)], xb[1, k]
            ).astype(BF16)
            columns = pl.ds(pl.multiple_of(k * 512, 512), 512)
            yso[2 * h, :, columns] = part[:128]
            yso[2 * h + 1, :, columns] = part[128:]

        for d in near_first:
            start(y_send(ATTN, d))

    def projection_term(a):
        @pl.loop(0, 4)
        def _(i):
            k, h = i // 2, i % 2
            part = contract_rows(
                xb[0, k, :, pl.ds(pl.multiple_of(h * 256, 256), 256)], gb[a]
            ).astype(BF16)
            rows = pl.ds(pl.multiple_of(i * 256, 256), 256)
            for q in range(4):
                ys[a, q, rows] = part[:, q * 128 : (q + 1) * 128]

        for d in near_first:
            start(y_send(a, d))

    def z_slot(a):
        return zro.at[zh] if a == ATTN else zr.at[a, zh]

    def z_piece(a, k):
        return zso.at[k] if a == ATTN else zs.at[a, k]

    def z_far(a):
        return remote(z_piece(a, flip(zl1)), z_slot(a), dz_s.at[a, 0], dz_r.at[a, zh], device(zh_=zl1, zl_=zl_far))

    def z_over(a):
        return remote(z_piece(a, zl1), z_slot(a), dz_s.at[a, 1], dz_r.at[a, zh], over)

    def z_self(a):
        return pltpu.make_async_copy(z_piece(a, zl1), z_slot(a), dz_r.at[a, zh])

    def z_arrival(a, s):
        place = zro.at[s] if a == ATTN else zr.at[a, s]
        return remote(place, place, dz_s.at[a, 0], dz_r.at[a, s], far)

    def sum_y(a):
        for d in (0, 1, 2):
            y_send(a, d).wait_recv()
        if a == ATTN:
            for k in (0, 1):
                cols = slice(k * 512, (k + 1) * 512)
                total = yso[y, :, cols].astype(F32) + yro[0, :, cols].astype(F32)
                total = total + yro[1, :, cols].astype(F32) + yro[2, :, cols].astype(F32)
                zso[k] = total.astype(BF16)
        else:
            @pl.loop(0, 4)
            def _(i):
                rows = pl.ds(pl.multiple_of(i * 256, 256), 256)
                total = ys[a, y, rows].astype(F32) + yr[a, 0, rows].astype(F32)
                total = total + yr[a, 1, rows].astype(F32) + yr[a, 2, rows].astype(F32)
                zs[a, i // 2, pl.ds(pl.multiple_of((i % 2) * 256, 256), 256)] = total.astype(BF16)

        start(z_far(a))

        @pl.when(home)
        def _():
            z_self(a).start()

        @pl.when(jnp.logical_not(home))
        def _():
            z_over(a).start()

    def gi_part(s):
        return flip(zl1) if s == 0 else zl1

    def gi_send(s, d):
        return remote(xs.at[gi_part(s), (x + d + 1) % 4], xr.at[s, d], gx_s.at[s, d], gx_r.at[s, d], x_peer[d])

    def input_term(s):
        k = gi_part(s)

        @pl.loop(0, 4)
        def _(b):
            rows = bank(b)
            total = contract_columns(gb[0, rows], wb[0, k])
            total = total + contract_columns(gb[1, rows], wb[1, k])
            total = total + contract_columns(gb[2, rows], wb[2, k])
            xs[k, b] = total.astype(BF16)

        for d in near_first:
            start(gi_send(s, d))

    def gi_far():
        return remote(gzs, gz, gg_s, gg_r, far)

    def sum_x(s):
        for d in (0, 1, 2):
            gi_send(s, d).wait_recv()
        total = xs[gi_part(s), x].astype(F32) + xr[s, 0].astype(F32)
        return total + xr[s, 1].astype(F32) + xr[s, 2].astype(F32)

    pass_w(0)
    pass_g(ATTN)
    pass_x(1)
    pass_w(1)
    pass_x(0)
    have_g(ATTN)
    have_x(1)
    output_term()
    pass_w(2)
    pass_g(0)
    have_x(0)
    have_g(0)
    projection_term(0)
    pass_g(1)
    have_g(1)
    projection_term(1)
    sum_y(ATTN)
    pass_g(2)
    have_g(2)
    projection_term(2)
    for a in (0, 1, 2):
        for d in (0, 1, 2):
            w_pass(a, d).wait_recv()
    input_term(0)
    input_term(1)
    sum_y(0)
    sum_y(1)
    gzs[...] = sum_x(0).astype(BF16)
    start(gi_far())
    sum_y(2)
    ownv[...] = sum_x(1)
    own_out = pltpu.make_async_copy(ownv, gown, loc_sem.at[6])
    own_out.start()

    gi_far().wait_recv()
    for a in (ATTN, 0, 1, 2):
        for s in (0, 1):
            z_arrival(a, s).wait_recv()
    own_out.wait()
    for copy in sent:
        copy.wait_send()

    @pl.when(jnp.logical_not(home))
    def _():
        for a in (0, 1, 2):
            w_here(a).wait_send()
        for a in (0, 1, 2, 3):
            z_over(a).wait_send()


def finish_kernel(zr, zro, gz, gown, gi, dq, dk, dv, do):
    for a, out in enumerate((dq, dk, dv)):
        out[...] = zr[a, 0].astype(F32) + zr[a, 1].astype(F32)
    do[...] = zro[0].astype(F32) + zro[1].astype(F32)
    gi[...] = (gown[...] + gz[...].astype(F32)).astype(BF16)


def local(inputs, attn_out, grad_out, grad_query, grad_key, grad_value, query_weight, key_weight, value_weight):
    rows, wide, thin = 256, 512, 128
    sem = pltpu.SemaphoreType.DMA
    vm = pltpu.VMEM
    parts = pl.pallas_call(
        exchange_kernel,
        name="exchange",
        out_shape=(
            jax.ShapeDtypeStruct((3, 2, wide, thin), BF16),
            jax.ShapeDtypeStruct((2, thin, wide), BF16),
            jax.ShapeDtypeStruct((rows, wide), BF16),
            jax.ShapeDtypeStruct((rows, wide), F32),
        ),
        in_specs=[pl.BlockSpec(memory_space=pl.ANY)] * 9,
        out_specs=[pl.BlockSpec(memory_space=pl.ANY)] * 4,
        scratch_shapes=[
            vm((2, 2, 4 * rows, wide), BF16),
            vm((4, 4 * rows, wide), BF16),
            vm((3, 2, wide, wide), BF16),
            vm((3, 4, 2 * wide, thin), BF16),
            vm((4, thin, 2 * wide), BF16),
            vm((3, 3, 2 * wide, thin), BF16),
            vm((3, thin, 2 * wide), BF16),
            vm((3, 2, wide, thin), BF16),
            vm((2, thin, wide), BF16),
            vm((2, 4, rows, wide), BF16),
            vm((2, 3, rows, wide), BF16),
            vm((rows, wide), BF16),
            vm((rows, wide), F32),
            sem((7,)),
            sem((2,)), sem((2,)),
            sem((2, 3)), sem((2, 3)),
            sem((2, 3)), sem((2, 3)),
            sem((4,)), sem((4,)),
            sem((4,)), sem((4,)),
            sem((4,)), sem((4,)),
            sem((3, 2)), sem((3, 2)),
            sem((3, 3)), sem((3, 3)),
            sem((4, 3)), sem((4, 3)),
            sem((4, 2)), sem((4, 2)),
            sem((2, 3)), sem((2, 3)),
            sem, sem,
        ],
        compiler_params=pltpu.CompilerParams(
            collective_id=0, has_side_effects=True, vmem_limit_bytes=56 * 2**20
        ),
    )(
        inputs.reshape(rows, wide),
        grad_out.reshape(rows, wide),
        grad_query.reshape(4 * rows, thin),
        grad_key.reshape(4 * rows, thin),
        grad_value.reshape(4 * rows, thin),
        attn_out.reshape(4 * rows, thin),
        query_weight,
        key_weight,
        value_weight,
    )
    gi, dq, dk, dv, do = pl.pallas_call(
        finish_kernel,
        name="finish",
        out_shape=(
            jax.ShapeDtypeStruct((rows, wide), BF16),
            jax.ShapeDtypeStruct((wide, thin), F32),
            jax.ShapeDtypeStruct((wide, thin), F32),
            jax.ShapeDtypeStruct((wide, thin), F32),
            jax.ShapeDtypeStruct((thin, wide), F32),
        ),
        compiler_params=pltpu.CompilerParams(vmem_limit_bytes=32 * 2**20),
    )(*parts)
    return gi.reshape(inputs.shape), dq, dk, dv, do


def solution(mesh):
    return jax.shard_map(
        local,
        mesh=mesh,
        in_specs=(
            P("ia", "ja", "ka"),
            P(None, "ja", ("ia", "ka")),
            P("ia", "ja", "ka"),
            P(None, "ja", ("ia", "ka")),
            P(None, "ja", ("ia", "ka")),
            P(None, "ja", ("ia", "ka")),
            P("ka", ("ia", "ja")),
            P("ka", ("ia", "ja")),
            P("ka", ("ia", "ja")),
        ),
        out_specs=(
            P("ia", "ja", "ka"),
            P("ka", ("ia", "ja")),
            P("ka", ("ia", "ja")),
            P("ka", ("ia", "ja")),
            P(("ia", "ja"), "ka"),
        ),
        check_vma=False,
    )
```

```python
import functools

import jax
import jax.numpy as jnp
from jax import lax
from jax.experimental import pallas as pl
from jax.experimental.pallas import tpu as pltpu
from jax.sharding import PartitionSpec as P

MESH = pl.DeviceIdType.MESH
BF16 = jnp.bfloat16
F32 = jnp.float32
ATTN = 3


def contract_rows(a, b):
    return lax.dot_general(a, b, (((0,), (0,)), ((), ())), preferred_element_type=F32)


def contract_columns(a, b):
    return lax.dot_general(a, b, (((1,), (1,)), ((), ())), preferred_element_type=F32)


def exchange_kernel(
    in_ref, go_ref, gq_ref, gk_ref, gv_ref, at_ref, wq_ref, wk_ref, wv_ref,
    zr, zro, gz, gown,
    xb, gb, wb, wr, zw, zwo, ys, yso, ya, yao, yr, yro, zs, zso, xs, xa, xr, gzs, ownv,
    loc_sem, xz_s, xz_r, xo_s, xo_r,
    gz_s, gz_r, gc_s, gc_r, gf_s, gf_r,
    wz_s, wz_r, wy_s, wy_r, dy_s, dy_r, dz_s, dz_r,
    gx_s, gx_r, gg_s, gg_r, wr_r, zw_r,
):
    ia, ja, ka = lax.axis_index("ia"), lax.axis_index("ja"), lax.axis_index("ka")
    x, y, zh = ia, ja % 4, ja // 4
    zl, c = ka // 2, ka % 2
    zl1, zl0 = zl // 2, zl % 2

    def device(x_=None, y_=None, zh_=None, zl_=None, c_=None):
        x_ = x if x_ is None else x_
        y_ = y if y_ is None else y_
        zh_ = zh if zh_ is None else zh_
        zl_ = zl if zl_ is None else zl_
        c_ = c if c_ is None else c_
        return (x_, zh_ * 4 + y_, zl_ * 2 + c_)

    def flip(bit):
        return 1 - bit

    def around(i, d):
        return (i + d) % 4

    zl_side = zl1 * 2 + flip(zl0)
    zl_far = flip(zl1) * 2 + zl0
    side, far, core = device(zl_=zl_side), device(zl_=zl_far), device(c_=flip(c))
    over_far = device(zh_=flip(zh), zl_=zl_far)
    x_up, x_down = device(x_=around(x, 1)), device(x_=around(x, 3))
    y_up, y_down = device(y_=around(y, 1)), device(y_=around(y, 3))

    def remote(src, dst, send, recv, to):
        return pltpu.make_async_remote_copy(
            src_ref=src, dst_ref=dst, send_sem=send, recv_sem=recv,
            device_id=to, device_id_type=MESH,
        )

    sent, seen = [], set()

    def start(copy):
        copy.start()
        sent.append(copy)

    def once(key, wait):
        if key not in seen:
            seen.add(key)
            wait()

    def lanes(k):
        return pl.ds(pl.multiple_of(k * 128, 128), 128)

    def bank(b):
        return pl.ds(pl.multiple_of(b * 256, 256), 256)

    g_refs = (gq_ref, gk_ref, gv_ref, at_ref)
    w_refs = (wq_ref, wk_ref, wv_ref)
    x_refs = (in_ref, go_ref)
    k_own, k_side = zl0 * 2 + c, flip(zl0) * 2 + c

    def own_g(a):
        return pltpu.make_async_copy(g_refs[a], gb.at[a, :, lanes(k_own)], loc_sem.at[a])

    def own_x(t):
        return pltpu.make_async_copy(x_refs[t], xb.at[t, zl1, bank(x)], loc_sem.at[4 + t])

    def g_side(a):
        return remote(g_refs[a], gb.at[a, :, lanes(k_own)], gz_s.at[a], gz_r.at[a], side)

    def g_core(a):
        return remote(g_refs[a], gb.at[a, :, lanes(k_own)], gc_s.at[a], gc_r.at[a], core)

    def g_pass(a):
        place = gb.at[a, :, lanes(k_side)]
        return remote(place, place, gf_s.at[a], gf_r.at[a], core)

    def send_g(a):
        start(g_side(a))
        start(g_core(a))

    def pass_g(a):
        g_side(a).wait_recv()
        start(g_pass(a))

    def have_g(a):
        def wait():
            own_g(a).wait()
            g_core(a).wait_recv()
            g_pass(a).wait_recv()

        once(("g", a), wait)

    def x_far(t):
        return remote(x_refs[t], xb.at[t, zl1, bank(x)], xz_s.at[t], xz_r.at[t], far)

    def x_ring(t, j):
        if j < 2:
            src, dst = x_refs[t], xb.at[t, zl1, bank(x)]
        elif j < 4:
            src = dst = xb.at[t, flip(zl1), bank(x)]
        elif j == 4:
            src = dst = xb.at[t, zl1, bank(around(x, 3))]
        else:
            src = dst = xb.at[t, flip(zl1), bank(around(x, 1))]
        return remote(src, dst, xo_s.at[t, j], xo_r.at[t, j], x_down if j % 2 else x_up)

    def send_far(t):
        start(x_far(t))

    def send_x(t):
        start(x_ring(t, 0))
        start(x_ring(t, 1))

    def pass_x(t):
        x_far(t).wait_recv()
        start(x_ring(t, 2))
        start(x_ring(t, 3))

    def forward_own(t):
        x_ring(t, 0).wait_recv()
        start(x_ring(t, 4))

    def forward_far(t):
        x_ring(t, 3).wait_recv()
        start(x_ring(t, 5))

    def have_x(t):
        def wait():
            own_x(t).wait()
            for j in (1, 2, 4, 5):
                x_ring(t, j).wait_recv()

        once(("x", t), wait)

    home = zl1 == zh
    away = jnp.logical_not(home)

    def w_place(a, k):
        return wb.at[a, k, :, lanes(y)]

    def w_first(a, dst, recv):
        return remote(w_refs[a], dst, wz_s.at[a, 0], recv, over_far)

    def w_first_home(a):
        return w_first(a, wr.at[a], wr_r.at[a])

    def w_first_away(a):
        return w_first(a, w_place(a, zl1), wz_r.at[a, zl1])

    def w_second_home(a):
        return remote(wr.at[a], w_place(a, flip(zl1)), wz_s.at[a, 1], wz_r.at[a, flip(zl1)], far)

    def w_second_away(a):
        return remote(w_refs[a], w_place(a, zl1), wz_s.at[a, 1], wz_r.at[a, zl1], far)

    def w_self(a):
        return pltpu.make_async_copy(w_refs[a], w_place(a, zl1), wz_r.at[a, zl1])

    def w_arrival(a, k):
        return remote(w_place(a, k), w_place(a, k), wz_s.at[a, 0], wz_r.at[a, k], far)

    def w_ring(a, j):
        if j < 2:
            place = wb.at[a, :, :, lanes(y)]
        elif j == 2:
            place = wb.at[a, 0, :, lanes(around(y, 3))]
        else:
            place = wb.at[a, 1, :, lanes(around(y, 1))]
        return remote(place, place, wy_s.at[a, j], wy_r.at[a, j], y_down if j % 2 else y_up)

    def send_w(a):
        @pl.when(home)
        def _():
            w_first_home(a).start()
            w_self(a).start()

        @pl.when(away)
        def _():
            w_first_away(a).start()
            w_second_away(a).start()

    def relay_w(a):
        @pl.when(home)
        def _():
            w_first_home(a).wait_recv()
            w_second_home(a).start()

    def pass_w(a):
        for k in (0, 1):
            w_arrival(a, k).wait_recv()
        start(w_ring(a, 0))
        start(w_ring(a, 1))

    def forward_w(a):
        w_ring(a, 0).wait_recv()
        w_ring(a, 1).wait_recv()
        start(w_ring(a, 2))
        start(w_ring(a, 3))

    def have_w(a):
        def wait():
            for j in (2, 3):
                w_ring(a, j).wait_recv()

        once(("w", a), wait)

    def ring_copy(me, up, down, piece, relay, result, send, recv, j):
        if j == 0:
            src, dst = piece(around(me, 2), 0), relay(0)
        elif j == 1:
            src, dst = piece(around(me, 2), 1), relay(1)
        elif j == 2:
            src, dst = piece(around(me, 1), 1), result(0, 1)
        elif j == 3:
            src, dst = piece(around(me, 3), 0), result(1, 0)
        elif j == 4:
            src, dst = piece(around(me, 1), 0), result(0, 0)
        else:
            src, dst = piece(around(me, 3), 1), result(1, 1)
        return remote(src, dst, send(j), recv(j), down if j % 2 else up)

    def ring_add(me, piece, relay):
        for h, d in ((0, 1), (1, 3)):
            place = piece(around(me, d), h)
            place[...] = (place[...].astype(F32) + relay(h)[...].astype(F32)).astype(BF16)

    def ring_total(me, piece, result, h):
        total = piece(me, h)[...].astype(F32) + result(0, h)[...].astype(F32)
        return total + result(1, h)[...].astype(F32)

    def y_piece(a):
        if a == ATTN:
            return lambda q, h: yso.at[q, h]
        return lambda q, h: ys.at[a, q, h]

    def y_relay(a):
        return (lambda h: yao.at[h]) if a == ATTN else (lambda h: ya.at[a, h])

    def y_result(a):
        if a == ATTN:
            return lambda d, h: yro.at[d, h]
        return lambda d, h: yr.at[a, d, h]

    def y_copy(a, j):
        return ring_copy(
            y, y_up, y_down, y_piece(a), y_relay(a), y_result(a),
            lambda i: dy_s.at[a, i], lambda i: dy_r.at[a, i], j,
        )

    def term(a):
        have_x(1 if a == ATTN else 0)
        have_g(a)

        @pl.loop(0, 4)
        def _(i):
            k, h = i // 2, i % 2
            part = pl.ds(pl.multiple_of(h * 256, 256), 256)
            if a == ATTN:
                block = contract_rows(gb[ATTN, :, part], xb[1, k]).astype(BF16)
                yso[2 * h, k] = block[:128]
                yso[2 * h + 1, k] = block[128:]
            else:
                block = contract_rows(xb[0, k, :, part], gb[a]).astype(BF16)
                for q in range(4):
                    ys[a, q, k, part] = block[:, q * 128 : (q + 1) * 128]

        for j in range(4):
            start(y_copy(a, j))

    def combine(a):
        y_copy(a, 0).wait_recv()
        y_copy(a, 1).wait_recv()
        ring_add(y, y_piece(a), y_relay(a))
        start(y_copy(a, 4))
        start(y_copy(a, 5))

    def z_slot(a):
        return zro.at[zh] if a == ATTN else zr.at[a, zh]

    def z_piece(a, k):
        return zso.at[k] if a == ATTN else zs.at[a, k]

    def z_relay(a):
        return zwo if a == ATTN else zw.at[a]

    def z_far_home(a):
        return remote(z_piece(a, flip(zl1)), z_slot(a), dz_s.at[a, 0], dz_r.at[a, zh], far)

    def z_far_away(a):
        return remote(z_piece(a, zl1), z_relay(a), dz_s.at[a, 0], zw_r.at[a], far)

    def z_over_home(a):
        return remote(z_relay(a), z_slot(a), dz_s.at[a, 1], dz_r.at[a, zh], over_far)

    def z_over_away(a):
        return remote(z_piece(a, flip(zl1)), z_slot(a), dz_s.at[a, 1], dz_r.at[a, zh], over_far)

    def z_self(a):
        return pltpu.make_async_copy(z_piece(a, zl1), z_slot(a), dz_r.at[a, zh])

    def z_arrival(a, s):
        place = zro.at[s] if a == ATTN else zr.at[a, s]
        return remote(place, place, dz_s.at[a, 0], dz_r.at[a, s], far)

    def sum_y(a):
        for j in range(2, 6):
            y_copy(a, j).wait_recv()
        for h in (0, 1):
            z_piece(a, h)[...] = ring_total(y, y_piece(a), y_result(a), h).astype(BF16)

        @pl.when(home)
        def _():
            z_far_home(a).start()
            z_self(a).start()

        @pl.when(away)
        def _():
            z_far_away(a).start()
            z_over_away(a).start()

    def relay_z(a):
        @pl.when(home)
        def _():
            z_far_away(a).wait_recv()
            z_over_home(a).start()

    def gi_part(s):
        return flip(zl1) if s == 0 else zl1

    def gi_piece(s):
        return lambda b, h: xs.at[gi_part(s), b, h]

    def gi_copy(s, j):
        return ring_copy(
            x, x_up, x_down, gi_piece(s), lambda h: xa.at[s, h], lambda d, h: xr.at[s, d, h],
            lambda i: gx_s.at[s, i], lambda i: gx_r.at[s, i], j,
        )

    def input_term(s):
        for a in (0, 1, 2):
            have_g(a)
            have_w(a)
        k = gi_part(s)

        @pl.loop(0, 4)
        def _(b):
            rows = bank(b)
            total = contract_columns(gb[0, rows], wb[0, k])
            total = total + contract_columns(gb[1, rows], wb[1, k])
            total = total + contract_columns(gb[2, rows], wb[2, k])
            xs[k, b, 0] = total[:128].astype(BF16)
            xs[k, b, 1] = total[128:].astype(BF16)

        for j in range(4):
            start(gi_copy(s, j))

    def gi_combine(s):
        gi_copy(s, 0).wait_recv()
        gi_copy(s, 1).wait_recv()
        ring_add(x, gi_piece(s), lambda h: xa.at[s, h])
        start(gi_copy(s, 4))
        start(gi_copy(s, 5))

    def gi_far():
        return remote(gzs, gz, gg_s, gg_r, far)

    own_out = pltpu.make_async_copy(ownv, gown, loc_sem.at[6])

    def sum_x(s):
        for j in range(2, 6):
            gi_copy(s, j).wait_recv()
        for h in (0, 1):
            total = ring_total(x, gi_piece(s), lambda d, i: xr.at[s, d, i], h)
            rows = slice(h * 128, (h + 1) * 128)
            if s == 0:
                gzs[rows] = total.astype(BF16)
            else:
                ownv[rows] = total
        if s == 0:
            start(gi_far())
        else:
            own_out.start()

    for a in (0, 1, 2, ATTN):
        own_g(a).start()
    for t in (0, 1):
        own_x(t).start()

    barrier = pltpu.get_barrier_semaphore()
    peers = [x_up, x_down, y_up, y_down, side, far, core, over_far]
    for peer in peers:
        pl.semaphore_signal(barrier, inc=1, device_id=peer, device_id_type=MESH)
    pl.semaphore_wait(barrier, len(peers))

    send_far(0)
    send_w(0)
    send_w(1)
    send_x(1)
    relay_w(0)
    send_x(0)
    send_w(2)
    relay_w(1)
    send_g(0)
    pass_x(0)
    forward_own(1)
    forward_own(0)
    pass_w(0)
    send_g(2)
    relay_w(2)
    pass_w(1)
    send_far(1)
    forward_w(0)
    forward_far(0)
    pass_g(0)
    forward_w(1)
    pass_w(2)
    send_g(1)
    term(0)
    send_g(ATTN)
    pass_x(1)
    pass_g(2)
    forward_w(2)
    combine(0)
    pass_g(1)
    term(1)
    forward_far(1)
    pass_g(ATTN)
    input_term(0)
    input_term(1)
    combine(1)
    sum_y(0)
    term(2)
    combine(2)
    sum_y(1)
    term(ATTN)
    relay_z(0)
    sum_y(2)
    gi_combine(1)
    combine(ATTN)
    relay_z(1)
    gi_combine(0)
    sum_y(ATTN)
    sum_x(1)
    sum_x(0)
    relay_z(2)
    relay_z(ATTN)

    gi_far().wait_recv()
    for a in (0, 1, 2, ATTN):
        for s in (0, 1):
            z_arrival(a, s).wait_recv()
    own_out.wait()
    for copy in sent:
        copy.wait_send()

    @pl.when(home)
    def _():
        for a in (0, 1, 2):
            w_first_home(a).wait_send()
            w_second_home(a).wait_send()
        for a in (0, 1, 2, ATTN):
            z_far_home(a).wait_send()
            z_over_home(a).wait_send()

    @pl.when(away)
    def _():
        for a in (0, 1, 2):
            w_first_away(a).wait_send()
            w_second_away(a).wait_send()
        for a in (0, 1, 2, ATTN):
            z_far_away(a).wait_send()
            z_over_away(a).wait_send()


def finish_kernel(zr_hbm, zro_hbm, gz_hbm, gown_hbm, gi, dq, dk, dv, do, zr, zro, gz, gown, sems):
    pairs = ((zr_hbm, zr), (zro_hbm, zro), (gz_hbm, gz), (gown_hbm, gown))
    copies = [pltpu.make_async_copy(src, dst, sems.at[i]) for i, (src, dst) in enumerate(pairs)]
    for copy in copies:
        copy.start()
    for copy in copies:
        copy.wait()
    for a, out in enumerate((dq, dk, dv)):
        out[...] = zr[a, 0].astype(F32) + zr[a, 1].astype(F32)
    do[...] = zro[0].astype(F32) + zro[1].astype(F32)
    gi[...] = (gown[...] + gz[...].astype(F32)).astype(BF16)


def local(inputs, attn_out, grad_out, grad_query, grad_key, grad_value, query_weight, key_weight, value_weight):
    rows, wide, thin = 256, 512, 128
    sem = pltpu.SemaphoreType.DMA
    vm = pltpu.VMEM
    parts = pl.pallas_call(
        exchange_kernel,
        name="exchange",
        out_shape=(
            jax.ShapeDtypeStruct((3, 2, wide, thin), BF16),
            jax.ShapeDtypeStruct((2, thin, wide), BF16),
            jax.ShapeDtypeStruct((rows, wide), BF16),
            jax.ShapeDtypeStruct((rows, wide), F32),
        ),
        in_specs=[pl.BlockSpec(memory_space=pl.ANY)] * 9,
        out_specs=[pl.BlockSpec(memory_space=pl.ANY)] * 4,
        scratch_shapes=[
            vm((2, 2, 4 * rows, wide), BF16),
            vm((4, 4 * rows, wide), BF16),
            vm((3, 2, wide, wide), BF16),
            vm((3, wide, thin), BF16),
            vm((3, wide, thin), BF16),
            vm((thin, wide), BF16),
            vm((3, 4, 2, wide, thin), BF16),
            vm((4, 2, thin, wide), BF16),
            vm((3, 2, wide, thin), BF16),
            vm((2, thin, wide), BF16),
            vm((3, 2, 2, wide, thin), BF16),
            vm((2, 2, thin, wide), BF16),
            vm((3, 2, wide, thin), BF16),
            vm((2, thin, wide), BF16),
            vm((2, 4, 2, thin, wide), BF16),
            vm((2, 2, thin, wide), BF16),
            vm((2, 2, 2, thin, wide), BF16),
            vm((rows, wide), BF16),
            vm((rows, wide), F32),
            sem((7,)),
            sem((2,)), sem((2,)),
            sem((2, 6)), sem((2, 6)),
            sem((4,)), sem((4,)),
            sem((4,)), sem((4,)),
            sem((4,)), sem((4,)),
            sem((3, 2)), sem((3, 2)),
            sem((3, 4)), sem((3, 4)),
            sem((4, 6)), sem((4, 6)),
            sem((4, 2)), sem((4, 2)),
            sem((2, 6)), sem((2, 6)),
            sem, sem,
            sem((3,)), sem((4,)),
        ],
        compiler_params=pltpu.CompilerParams(
            collective_id=0, has_side_effects=True, vmem_limit_bytes=56 * 2**20
        ),
    )(
        inputs.reshape(rows, wide),
        grad_out.reshape(rows, wide),
        grad_query.reshape(4 * rows, thin),
        grad_key.reshape(4 * rows, thin),
        grad_value.reshape(4 * rows, thin),
        attn_out.reshape(4 * rows, thin),
        query_weight,
        key_weight,
        value_weight,
    )
    gi, dq, dk, dv, do = pl.pallas_call(
        finish_kernel,
        name="finish",
        out_shape=(
            jax.ShapeDtypeStruct((rows, wide), BF16),
            jax.ShapeDtypeStruct((wide, thin), F32),
            jax.ShapeDtypeStruct((wide, thin), F32),
            jax.ShapeDtypeStruct((wide, thin), F32),
            jax.ShapeDtypeStruct((thin, wide), F32),
        ),
        in_specs=[pl.BlockSpec(memory_space=pl.ANY)] * 4,
        scratch_shapes=[
            vm((3, 2, wide, thin), BF16),
            vm((2, thin, wide), BF16),
            vm((rows, wide), BF16),
            vm((rows, wide), F32),
            sem((4,)),
        ],
        compiler_params=pltpu.CompilerParams(vmem_limit_bytes=62 * 2**20),
    )(*parts)
    return gi.reshape(inputs.shape), dq, dk, dv, do


def solution(mesh):
    return jax.shard_map(
        local,
        mesh=mesh,
        in_specs=(
            P("ia", "ja", "ka"),
            P(None, "ja", ("ia", "ka")),
            P("ia", "ja", "ka"),
            P(None, "ja", ("ia", "ka")),
            P(None, "ja", ("ia", "ka")),
            P(None, "ja", ("ia", "ka")),
            P("ka", ("ia", "ja")),
            P("ka", ("ia", "ja")),
            P("ka", ("ia", "ja")),
        ),
        out_specs=(
            P("ia", "ja", "ka"),
            P("ka", ("ia", "ja")),
            P("ka", ("ia", "ja")),
            P("ka", ("ia", "ja")),
            P(("ia", "ja"), "ka"),
        ),
        check_vma=False,
    )
```

```python
import functools

import jax
import jax.numpy as jnp
from jax import lax
from jax.experimental import pallas as pl
from jax.experimental.pallas import tpu as pltpu
from jax.sharding import PartitionSpec as P

MESH = pl.DeviceIdType.MESH
BF16 = jnp.bfloat16
F32 = jnp.float32
ATTN = 3


def contract_rows(a, b):
    return lax.dot_general(a, b, (((0,), (0,)), ((), ())), preferred_element_type=F32)


def contract_columns(a, b):
    return lax.dot_general(a, b, (((1,), (1,)), ((), ())), preferred_element_type=F32)


def exchange_kernel(
    in_ref, go_ref, gq_ref, gk_ref, gv_ref, at_ref, wq_ref, wk_ref, wv_ref,
    zr, zro, gz, gown,
    xb, gb, wb, wr, zw, zwo, ys, yso, ya, yao, yr, yro, zs, zso, xs, xa, xr, gzs, ownv,
    loc_sem, xz_s, xz_r, xo_s, xo_r,
    gz_s, gz_r, gc_s, gc_r, gf_s, gf_r,
    wz_s, wz_r, wy_s, wy_r, dy_s, dy_r, dz_s, dz_r,
    gx_s, gx_r, gg_s, gg_r, wr_r, zw_r,
):
    ia, ja, ka = lax.axis_index("ia"), lax.axis_index("ja"), lax.axis_index("ka")
    x, y, zh = ia, ja % 4, ja // 4
    zl, c = ka // 2, ka % 2
    zl1, zl0 = zl // 2, zl % 2

    def device(x_=None, y_=None, zh_=None, zl_=None, c_=None):
        x_ = x if x_ is None else x_
        y_ = y if y_ is None else y_
        zh_ = zh if zh_ is None else zh_
        zl_ = zl if zl_ is None else zl_
        c_ = c if c_ is None else c_
        return (x_, zh_ * 4 + y_, zl_ * 2 + c_)

    def flip(bit):
        return 1 - bit

    def around(i, d):
        return (i + d) % 4

    zl_side = zl1 * 2 + flip(zl0)
    zl_far = flip(zl1) * 2 + zl0
    side, far, core = device(zl_=zl_side), device(zl_=zl_far), device(c_=flip(c))
    over_far = device(zh_=flip(zh), zl_=zl_far)
    x_up, x_down = device(x_=around(x, 1)), device(x_=around(x, 3))
    y_up, y_down = device(y_=around(y, 1)), device(y_=around(y, 3))

    def remote(src, dst, send, recv, to):
        return pltpu.make_async_remote_copy(
            src_ref=src, dst_ref=dst, send_sem=send, recv_sem=recv,
            device_id=to, device_id_type=MESH,
        )

    sent, seen = [], set()

    def start(copy):
        copy.start()
        sent.append(copy)

    def once(key, wait):
        if key not in seen:
            seen.add(key)
            wait()

    def lanes(k):
        return pl.ds(pl.multiple_of(k * 128, 128), 128)

    def bank(b):
        return pl.ds(pl.multiple_of(b * 256, 256), 256)

    g_refs = (gq_ref, gk_ref, gv_ref, at_ref)
    w_refs = (wq_ref, wk_ref, wv_ref)
    x_refs = (in_ref, go_ref)
    k_own, k_side = zl0 * 2 + c, flip(zl0) * 2 + c

    def own_g(a):
        return pltpu.make_async_copy(g_refs[a], gb.at[a, :, lanes(k_own)], loc_sem.at[a])

    def own_x(t):
        return pltpu.make_async_copy(x_refs[t], xb.at[t, zl1, bank(x)], loc_sem.at[4 + t])

    def g_side(a):
        return remote(g_refs[a], gb.at[a, :, lanes(k_own)], gz_s.at[a], gz_r.at[a], side)

    def g_core(a):
        return remote(g_refs[a], gb.at[a, :, lanes(k_own)], gc_s.at[a], gc_r.at[a], core)

    def g_pass(a):
        place = gb.at[a, :, lanes(k_side)]
        return remote(place, place, gf_s.at[a], gf_r.at[a], core)

    def send_g(a):
        start(g_side(a))
        start(g_core(a))

    def pass_g(a):
        g_side(a).wait_recv()
        start(g_pass(a))

    def have_g(a):
        def wait():
            own_g(a).wait()
            g_core(a).wait_recv()
            g_pass(a).wait_recv()

        once(("g", a), wait)

    def x_far(t):
        return remote(x_refs[t], xb.at[t, zl1, bank(x)], xz_s.at[t], xz_r.at[t], far)

    def x_ring(t, j):
        if j < 2:
            src, dst = x_refs[t], xb.at[t, zl1, bank(x)]
        elif j < 4:
            src = dst = xb.at[t, flip(zl1), bank(x)]
        elif j == 4:
            src = dst = xb.at[t, zl1, bank(around(x, 3))]
        else:
            src = dst = xb.at[t, flip(zl1), bank(around(x, 1))]
        return remote(src, dst, xo_s.at[t, j], xo_r.at[t, j], x_down if j % 2 else x_up)

    def send_far(t):
        start(x_far(t))

    def send_x(t):
        start(x_ring(t, 0))
        start(x_ring(t, 1))

    def pass_x(t):
        x_far(t).wait_recv()
        start(x_ring(t, 2))
        start(x_ring(t, 3))

    def forward_own(t):
        x_ring(t, 0).wait_recv()
        start(x_ring(t, 4))

    def forward_far(t):
        x_ring(t, 3).wait_recv()
        start(x_ring(t, 5))

    def have_x(t):
        def wait():
            own_x(t).wait()
            for j in (1, 2, 4, 5):
                x_ring(t, j).wait_recv()

        once(("x", t), wait)

    home = zl1 == zh
    away = jnp.logical_not(home)

    def w_place(a, k):
        return wb.at[a, k, :, lanes(y)]

    def w_first(a, dst, recv):
        return remote(w_refs[a], dst, wz_s.at[a, 0], recv, over_far)

    def w_first_home(a):
        return w_first(a, wr.at[a], wr_r.at[a])

    def w_first_away(a):
        return w_first(a, w_place(a, zl1), wz_r.at[a, zl1])

    def w_second_home(a):
        return remote(wr.at[a], w_place(a, flip(zl1)), wz_s.at[a, 1], wz_r.at[a, flip(zl1)], far)

    def w_second_away(a):
        return remote(w_refs[a], w_place(a, zl1), wz_s.at[a, 1], wz_r.at[a, zl1], far)

    def w_self(a):
        return pltpu.make_async_copy(w_refs[a], w_place(a, zl1), wz_r.at[a, zl1])

    def w_arrival(a, k):
        return remote(w_place(a, k), w_place(a, k), wz_s.at[a, 0], wz_r.at[a, k], far)

    def w_ring(a, j):
        if j < 2:
            place = wb.at[a, zh, :, lanes(y)]
        elif j < 4:
            place = wb.at[a, flip(zh), :, lanes(y)]
        elif j == 4:
            place = wb.at[a, zh, :, lanes(around(y, 3))]
        else:
            place = wb.at[a, flip(zh), :, lanes(around(y, 1))]
        return remote(place, place, wy_s.at[a, j], wy_r.at[a, j], y_down if j % 2 else y_up)

    def send_w(a):
        @pl.when(home)
        def _():
            w_first_home(a).start()
            w_self(a).start()

        @pl.when(away)
        def _():
            w_first_away(a).start()
            w_second_away(a).start()

    def relay_w(a):
        @pl.when(home)
        def _():
            w_first_home(a).wait_recv()
            w_second_home(a).start()

    def pass_first(a):
        w_arrival(a, zh).wait_recv()
        start(w_ring(a, 0))
        start(w_ring(a, 1))

    def pass_second(a):
        w_arrival(a, flip(zh)).wait_recv()
        start(w_ring(a, 2))
        start(w_ring(a, 3))

    def forward_first(a):
        w_ring(a, 0).wait_recv()
        start(w_ring(a, 4))

    def forward_second(a):
        w_ring(a, 3).wait_recv()
        start(w_ring(a, 5))

    def have_w(a):
        def wait():
            for j in (1, 2, 4, 5):
                w_ring(a, j).wait_recv()

        once(("w", a), wait)

    def ring_copy(me, up, down, piece, relay, result, send, recv, j):
        if j == 0:
            src, dst = piece(around(me, 2), 0), relay(0)
        elif j == 1:
            src, dst = piece(around(me, 2), 1), relay(1)
        elif j == 2:
            src, dst = piece(around(me, 1), 1), result(0, 1)
        elif j == 3:
            src, dst = piece(around(me, 3), 0), result(1, 0)
        elif j == 4:
            src, dst = piece(around(me, 1), 0), result(0, 0)
        else:
            src, dst = piece(around(me, 3), 1), result(1, 1)
        return remote(src, dst, send(j), recv(j), down if j % 2 else up)

    def ring_add(me, piece, relay):
        for h, d in ((0, 1), (1, 3)):
            place = piece(around(me, d), h)
            place[...] = (place[...].astype(F32) + relay(h)[...].astype(F32)).astype(BF16)

    def ring_total(me, piece, result, h):
        total = piece(me, h)[...].astype(F32) + result(0, h)[...].astype(F32)
        return total + result(1, h)[...].astype(F32)

    def y_piece(a, s):
        if a == ATTN:
            return lambda q, h: yso.at[q, s, h]
        return lambda q, h: ys.at[a, q, s, h]

    def y_relay(a, s):
        return (lambda h: yao.at[s, h]) if a == ATTN else (lambda h: ya.at[a, s, h])

    def y_result(a, s):
        if a == ATTN:
            return lambda d, h: yro.at[s, d, h]
        return lambda d, h: yr.at[a, s, d, h]

    def y_copy(a, s, j):
        return ring_copy(
            y, y_up, y_down, y_piece(a, s), y_relay(a, s), y_result(a, s),
            lambda i: dy_s.at[a * 2 + s, i], lambda i: dy_r.at[a * 2 + s, i], j,
        )

    def term(a, s):
        have_x(1 if a == ATTN else 0)
        have_g(a)
        part = slice(s * 256, (s + 1) * 256)

        @pl.loop(0, 2)
        def _(k):
            if a == ATTN:
                block = contract_rows(gb[ATTN], xb[1, k, :, part]).astype(BF16)
                for q in range(4):
                    yso[q, s, k] = block[q * 128 : (q + 1) * 128]
            else:
                block = contract_rows(xb[0, k, :, part], gb[a]).astype(BF16)
                for q in range(4):
                    ys[a, q, s, k] = block[:, q * 128 : (q + 1) * 128]

        for j in range(4):
            start(y_copy(a, s, j))

    def combine(a, s):
        y_copy(a, s, 0).wait_recv()
        y_copy(a, s, 1).wait_recv()
        ring_add(y, y_piece(a, s), y_relay(a, s))
        start(y_copy(a, s, 4))
        start(y_copy(a, s, 5))

    def z_place(a, s, slot):
        part = pl.ds(s * 256, 256)
        return zro.at[slot, :, part] if a == ATTN else zr.at[a, slot, part]

    def z_piece(a, s, k):
        return zso.at[s, k] if a == ATTN else zs.at[a, s, k]

    def z_relay(a, s):
        return zwo.at[s] if a == ATTN else zw.at[a, s]

    def z_copy(a, s, i, src, dst, recv, to):
        return remote(src, dst, dz_s.at[a * 2 + s, i], recv, to)

    def z_sem(a, s):
        return dz_r.at[a * 2 + s, zh]

    def z_far_home(a, s):
        return z_copy(a, s, 0, z_piece(a, s, flip(zl1)), z_place(a, s, zh), z_sem(a, s), far)

    def z_far_away(a, s):
        return z_copy(a, s, 0, z_piece(a, s, zl1), z_relay(a, s), zw_r.at[a * 2 + s], far)

    def z_over_home(a, s):
        return z_copy(a, s, 1, z_relay(a, s), z_place(a, s, zh), z_sem(a, s), over_far)

    def z_over_away(a, s):
        return z_copy(a, s, 1, z_piece(a, s, flip(zl1)), z_place(a, s, zh), z_sem(a, s), over_far)

    def z_self(a, s):
        return pltpu.make_async_copy(z_piece(a, s, zl1), z_place(a, s, zh), z_sem(a, s))

    def z_arrival(a, s, slot):
        place = z_place(a, s, slot)
        return remote(place, place, dz_s.at[a * 2 + s, 0], dz_r.at[a * 2 + s, slot], far)

    def sum_y(a, s):
        for j in range(2, 6):
            y_copy(a, s, j).wait_recv()
        for h in (0, 1):
            total = ring_total(y, y_piece(a, s), y_result(a, s), h)
            z_piece(a, s, h)[...] = total.astype(BF16)

        @pl.when(home)
        def _():
            z_far_home(a, s).start()
            z_self(a, s).start()

        @pl.when(away)
        def _():
            z_far_away(a, s).start()
            z_over_away(a, s).start()

    def relay_z(a, s):
        @pl.when(home)
        def _():
            z_far_away(a, s).wait_recv()
            z_over_home(a, s).start()

    def gi_part(s):
        return flip(zl1) if s == 0 else zl1

    def gi_piece(s):
        return lambda b, h: xs.at[gi_part(s), b, h]

    def gi_copy(s, j):
        return ring_copy(
            x, x_up, x_down, gi_piece(s), lambda h: xa.at[s, h], lambda d, h: xr.at[s, d, h],
            lambda i: gx_s.at[s, i], lambda i: gx_r.at[s, i], j,
        )

    def input_term(s):
        for a in (0, 1, 2):
            have_g(a)
            have_w(a)
        k = gi_part(s)

        @pl.loop(0, 4)
        def _(b):
            rows = bank(b)
            total = contract_columns(gb[0, rows], wb[0, k])
            total = total + contract_columns(gb[1, rows], wb[1, k])
            total = total + contract_columns(gb[2, rows], wb[2, k])
            xs[k, b, 0] = total[:128].astype(BF16)
            xs[k, b, 1] = total[128:].astype(BF16)

        for j in range(4):
            start(gi_copy(s, j))

    def gi_combine(s):
        gi_copy(s, 0).wait_recv()
        gi_copy(s, 1).wait_recv()
        ring_add(x, gi_piece(s), lambda h: xa.at[s, h])
        start(gi_copy(s, 4))
        start(gi_copy(s, 5))

    def gi_far():
        return remote(gzs, gz, gg_s, gg_r, far)

    own_out = pltpu.make_async_copy(ownv, gown, loc_sem.at[6])

    def sum_x(s):
        for j in range(2, 6):
            gi_copy(s, j).wait_recv()
        for h in (0, 1):
            total = ring_total(x, gi_piece(s), lambda d, i: xr.at[s, d, i], h)
            rows = slice(h * 128, (h + 1) * 128)
            if s == 0:
                gzs[rows] = total.astype(BF16)
            else:
                ownv[rows] = total
        if s == 0:
            start(gi_far())
        else:
            own_out.start()

    for a in (0, 1, 2, ATTN):
        own_g(a).start()
    for t in (0, 1):
        own_x(t).start()

    barrier = pltpu.get_barrier_semaphore()
    peers = [x_up, x_down, y_up, y_down, side, far, core, over_far]
    for peer in peers:
        pl.semaphore_signal(barrier, inc=1, device_id=peer, device_id_type=MESH)
    pl.semaphore_wait(barrier, len(peers))

    send_far(0)
    send_w(2)
    send_x(0)
    send_w(0)
    send_w(1)
    relay_w(2)
    relay_w(0)
    pass_first(2)
    pass_x(0)
    forward_own(0)
    pass_first(0)
    relay_w(1)
    send_x(1)
    pass_second(2)
    pass_first(1)
    send_g(2)
    send_g(1)
    send_far(1)
    forward_far(0)
    forward_first(2)
    pass_second(0)
    forward_first(1)
    forward_first(0)
    forward_second(2)
    pass_second(1)
    send_g(0)
    forward_second(0)
    forward_own(1)
    pass_g(2)
    send_g(ATTN)
    forward_second(1)
    term(2, 0)
    term(2, 1)
    pass_g(1)
    combine(2, 1)
    term(1, 1)
    pass_x(1)
    combine(2, 0)
    term(1, 0)
    pass_g(0)
    combine(1, 1)
    combine(1, 0)
    sum_y(2, 1)
    forward_far(1)
    sum_y(2, 0)
    term(0, 1)
    sum_y(1, 1)
    term(0, 0)
    pass_g(ATTN)
    combine(0, 1)
    input_term(0)
    combine(0, 0)
    term(ATTN, 0)
    sum_y(1, 0)
    relay_z(1, 1)
    relay_z(2, 0)
    term(ATTN, 1)
    sum_y(0, 0)
    gi_combine(0)
    relay_z(2, 1)
    sum_y(0, 1)
    combine(ATTN, 0)
    input_term(1)
    combine(ATTN, 1)
    sum_y(ATTN, 0)
    relay_z(0, 0)
    sum_y(ATTN, 1)
    gi_combine(1)
    relay_z(0, 1)
    sum_x(0)
    relay_z(ATTN, 0)
    relay_z(1, 0)
    relay_z(ATTN, 1)
    sum_x(1)

    gi_far().wait_recv()
    for a in (0, 1, 2, ATTN):
        for s in (0, 1):
            for slot in (0, 1):
                z_arrival(a, s, slot).wait_recv()
    own_out.wait()
    for copy in sent:
        copy.wait_send()

    @pl.when(home)
    def _():
        for a in (0, 1, 2):
            w_first_home(a).wait_send()
            w_second_home(a).wait_send()
        for a in (0, 1, 2, ATTN):
            for s in (0, 1):
                z_far_home(a, s).wait_send()
                z_over_home(a, s).wait_send()

    @pl.when(away)
    def _():
        for a in (0, 1, 2):
            w_first_away(a).wait_send()
            w_second_away(a).wait_send()
        for a in (0, 1, 2, ATTN):
            for s in (0, 1):
                z_far_away(a, s).wait_send()
                z_over_away(a, s).wait_send()


def finish_kernel(zr_hbm, zro_hbm, gz_hbm, gown_hbm, gi, dq, dk, dv, do, zr, zro, gz, gown, sems):
    pairs = ((zr_hbm, zr), (zro_hbm, zro), (gz_hbm, gz), (gown_hbm, gown))
    copies = [pltpu.make_async_copy(src, dst, sems.at[i]) for i, (src, dst) in enumerate(pairs)]
    for copy in copies:
        copy.start()
    for copy in copies:
        copy.wait()
    for a, out in enumerate((dq, dk, dv)):
        out[...] = zr[a, 0].astype(F32) + zr[a, 1].astype(F32)
    do[...] = zro[0].astype(F32) + zro[1].astype(F32)
    gi[...] = (gown[...] + gz[...].astype(F32)).astype(BF16)


def local(inputs, attn_out, grad_out, grad_query, grad_key, grad_value, query_weight, key_weight, value_weight):
    rows, wide, thin = 256, 512, 128
    sem = pltpu.SemaphoreType.DMA
    vm = pltpu.VMEM
    parts = pl.pallas_call(
        exchange_kernel,
        name="exchange",
        out_shape=(
            jax.ShapeDtypeStruct((3, 2, wide, thin), BF16),
            jax.ShapeDtypeStruct((2, thin, wide), BF16),
            jax.ShapeDtypeStruct((rows, wide), BF16),
            jax.ShapeDtypeStruct((rows, wide), F32),
        ),
        in_specs=[pl.BlockSpec(memory_space=pl.ANY)] * 9,
        out_specs=[pl.BlockSpec(memory_space=pl.ANY)] * 4,
        scratch_shapes=[
            vm((2, 2, 4 * rows, wide), BF16),
            vm((4, 4 * rows, wide), BF16),
            vm((3, 2, wide, wide), BF16),
            vm((3, wide, thin), BF16),
            vm((3, 2, rows, thin), BF16),
            vm((2, thin, rows), BF16),
            vm((3, 4, 2, 2, rows, thin), BF16),
            vm((4, 2, 2, thin, rows), BF16),
            vm((3, 2, 2, rows, thin), BF16),
            vm((2, 2, thin, rows), BF16),
            vm((3, 2, 2, 2, rows, thin), BF16),
            vm((2, 2, 2, thin, rows), BF16),
            vm((3, 2, 2, rows, thin), BF16),
            vm((2, 2, thin, rows), BF16),
            vm((2, 4, 2, thin, wide), BF16),
            vm((2, 2, thin, wide), BF16),
            vm((2, 2, 2, thin, wide), BF16),
            vm((rows, wide), BF16),
            vm((rows, wide), F32),
            sem((7,)),
            sem((2,)), sem((2,)),
            sem((2, 6)), sem((2, 6)),
            sem((4,)), sem((4,)),
            sem((4,)), sem((4,)),
            sem((4,)), sem((4,)),
            sem((3, 2)), sem((3, 2)),
            sem((3, 6)), sem((3, 6)),
            sem((8, 6)), sem((8, 6)),
            sem((8, 2)), sem((8, 2)),
            sem((2, 6)), sem((2, 6)),
            sem, sem,
            sem((3,)), sem((8,)),
        ],
        compiler_params=pltpu.CompilerParams(
            collective_id=0, has_side_effects=True, vmem_limit_bytes=56 * 2**20
        ),
    )(
        inputs.reshape(rows, wide),
        grad_out.reshape(rows, wide),
        grad_query.reshape(4 * rows, thin),
        grad_key.reshape(4 * rows, thin),
        grad_value.reshape(4 * rows, thin),
        attn_out.reshape(4 * rows, thin),
        query_weight,
        key_weight,
        value_weight,
    )
    gi, dq, dk, dv, do = pl.pallas_call(
        finish_kernel,
        name="finish",
        out_shape=(
            jax.ShapeDtypeStruct((rows, wide), BF16),
            jax.ShapeDtypeStruct((wide, thin), F32),
            jax.ShapeDtypeStruct((wide, thin), F32),
            jax.ShapeDtypeStruct((wide, thin), F32),
            jax.ShapeDtypeStruct((thin, wide), F32),
        ),
        in_specs=[pl.BlockSpec(memory_space=pl.ANY)] * 4,
        scratch_shapes=[
            vm((3, 2, wide, thin), BF16),
            vm((2, thin, wide), BF16),
            vm((rows, wide), BF16),
            vm((rows, wide), F32),
            sem((4,)),
        ],
        compiler_params=pltpu.CompilerParams(vmem_limit_bytes=62 * 2**20),
    )(*parts)
    return gi.reshape(inputs.shape), dq, dk, dv, do


def solution(mesh):
    return jax.shard_map(
        local,
        mesh=mesh,
        in_specs=(
            P("ia", "ja", "ka"),
            P(None, "ja", ("ia", "ka")),
            P("ia", "ja", "ka"),
            P(None, "ja", ("ia", "ka")),
            P(None, "ja", ("ia", "ka")),
            P(None, "ja", ("ia", "ka")),
            P("ka", ("ia", "ja")),
            P("ka", ("ia", "ja")),
            P("ka", ("ia", "ja")),
        ),
        out_specs=(
            P("ia", "ja", "ka"),
            P("ka", ("ia", "ja")),
            P("ka", ("ia", "ja")),
            P("ka", ("ia", "ja")),
            P(("ia", "ja"), "ka"),
        ),
        check_vma=False,
    )
```

```python
import functools

import jax
import jax.numpy as jnp
from jax import lax
from jax.experimental import pallas as pl
from jax.experimental.pallas import tpu as pltpu
from jax.sharding import PartitionSpec as P

MESH = pl.DeviceIdType.MESH
BF16 = jnp.bfloat16
F32 = jnp.float32
ATTN = 3


def contract_rows(a, b):
    return lax.dot_general(a, b, (((0,), (0,)), ((), ())), preferred_element_type=F32)


def contract_columns(a, b):
    return lax.dot_general(a, b, (((1,), (1,)), ((), ())), preferred_element_type=F32)


def exchange_kernel(
    in_ref, go_ref, gq_ref, gk_ref, gv_ref, at_ref, wq_ref, wk_ref, wv_ref,
    zr, zro, gz, gown,
    xb, gb, wb, wr, zw, zwo, ys, yso, ya, yao, yr, yro, zs, zso, xs, xa, xr, gzs, ownv,
    loc_sem, xz_s, xz_r, xo_s, xo_r,
    gz_s, gz_r, gc_s, gc_r, gf_s, gf_r,
    wz_s, wz_r, wy_s, wy_r, dy_s, dy_r, dz_s, dz_r,
    gx_s, gx_r, gg_s, gg_r, wr_r, zw_r,
):
    ia, ja, ka = lax.axis_index("ia"), lax.axis_index("ja"), lax.axis_index("ka")
    x, y, zh = ia, ja % 4, ja // 4
    zl, c = ka // 2, ka % 2
    zl1, zl0 = zl // 2, zl % 2

    def device(x_=None, y_=None, zh_=None, zl_=None, c_=None):
        x_ = x if x_ is None else x_
        y_ = y if y_ is None else y_
        zh_ = zh if zh_ is None else zh_
        zl_ = zl if zl_ is None else zl_
        c_ = c if c_ is None else c_
        return (x_, zh_ * 4 + y_, zl_ * 2 + c_)

    def flip(bit):
        return 1 - bit

    def around(i, d):
        return (i + d) % 4

    zl_side = zl1 * 2 + flip(zl0)
    zl_far = flip(zl1) * 2 + zl0
    side, far, core = device(zl_=zl_side), device(zl_=zl_far), device(c_=flip(c))
    over_far = device(zh_=flip(zh), zl_=zl_far)
    x_up, x_down = device(x_=around(x, 1)), device(x_=around(x, 3))
    y_up, y_down = device(y_=around(y, 1)), device(y_=around(y, 3))

    def remote(src, dst, send, recv, to):
        return pltpu.make_async_remote_copy(
            src_ref=src, dst_ref=dst, send_sem=send, recv_sem=recv,
            device_id=to, device_id_type=MESH,
        )

    sent, seen = [], set()

    def start(copy):
        copy.start()
        sent.append(copy)

    def once(key, wait):
        if key not in seen:
            seen.add(key)
            wait()

    def lanes(k):
        return pl.ds(pl.multiple_of(k * 128, 128), 128)

    def bank(b):
        return pl.ds(pl.multiple_of(b * 256, 256), 256)

    g_refs = (gq_ref, gk_ref, gv_ref, at_ref)
    w_refs = (wq_ref, wk_ref, wv_ref)
    x_refs = (in_ref, go_ref)
    k_own, k_side = zl0 * 2 + c, flip(zl0) * 2 + c

    def own_g(a):
        return pltpu.make_async_copy(g_refs[a], gb.at[a, :, lanes(k_own)], loc_sem.at[a])

    def own_x(t):
        return pltpu.make_async_copy(x_refs[t], xb.at[t, zl1, bank(x)], loc_sem.at[4 + t])

    def g_side(a):
        return remote(g_refs[a], gb.at[a, :, lanes(k_own)], gz_s.at[a], gz_r.at[a], side)

    def g_core(a):
        return remote(g_refs[a], gb.at[a, :, lanes(k_own)], gc_s.at[a], gc_r.at[a], core)

    def g_pass(a):
        place = gb.at[a, :, lanes(k_side)]
        return remote(place, place, gf_s.at[a], gf_r.at[a], core)

    def send_g(a):
        start(g_side(a))
        start(g_core(a))

    def pass_g(a):
        g_side(a).wait_recv()
        start(g_pass(a))

    def have_g(a):
        def wait():
            own_g(a).wait()
            g_core(a).wait_recv()
            g_pass(a).wait_recv()

        once(("g", a), wait)

    def x_far(t):
        return remote(x_refs[t], xb.at[t, zl1, bank(x)], xz_s.at[t], xz_r.at[t], far)

    def x_ring(t, j):
        if j < 2:
            src, dst = x_refs[t], xb.at[t, zl1, bank(x)]
        elif j < 4:
            src = dst = xb.at[t, flip(zl1), bank(x)]
        elif j == 4:
            src = dst = xb.at[t, zl1, bank(around(x, 3))]
        else:
            src = dst = xb.at[t, flip(zl1), bank(around(x, 1))]
        return remote(src, dst, xo_s.at[t, j], xo_r.at[t, j], x_down if j % 2 else x_up)

    def send_far(t):
        start(x_far(t))

    def send_x(t):
        start(x_ring(t, 0))
        start(x_ring(t, 1))

    def pass_x(t):
        x_far(t).wait_recv()
        start(x_ring(t, 2))
        start(x_ring(t, 3))

    def forward_own(t):
        x_ring(t, 0).wait_recv()
        start(x_ring(t, 4))

    def forward_far(t):
        x_ring(t, 3).wait_recv()
        start(x_ring(t, 5))

    def have_x(t):
        def wait():
            own_x(t).wait()
            for j in (1, 2, 4, 5):
                x_ring(t, j).wait_recv()

        once(("x", t), wait)

    home = zl1 == zh
    away = jnp.logical_not(home)

    def w_place(a, k):
        return wb.at[a, k, :, lanes(y)]

    def w_first(a, dst, recv):
        return remote(w_refs[a], dst, wz_s.at[a, 0], recv, over_far)

    def w_first_home(a):
        return w_first(a, wr.at[a], wr_r.at[a])

    def w_first_away(a):
        return w_first(a, w_place(a, zl1), wz_r.at[a, zl1])

    def w_second_home(a):
        return remote(wr.at[a], w_place(a, flip(zl1)), wz_s.at[a, 1], wz_r.at[a, flip(zl1)], far)

    def w_second_away(a):
        return remote(w_refs[a], w_place(a, zl1), wz_s.at[a, 1], wz_r.at[a, zl1], far)

    def w_self(a):
        return pltpu.make_async_copy(w_refs[a], w_place(a, zl1), wz_r.at[a, zl1])

    def w_arrival(a, k):
        return remote(w_place(a, k), w_place(a, k), wz_s.at[a, 0], wz_r.at[a, k], far)

    def w_ring(a, j):
        if j < 2:
            place = wb.at[a, zh, :, lanes(y)]
        elif j < 4:
            place = wb.at[a, flip(zh), :, lanes(y)]
        elif j == 4:
            place = wb.at[a, zh, :, lanes(around(y, 3))]
        else:
            place = wb.at[a, flip(zh), :, lanes(around(y, 1))]
        return remote(place, place, wy_s.at[a, j], wy_r.at[a, j], y_down if j % 2 else y_up)

    def send_w(a):
        @pl.when(home)
        def _():
            w_first_home(a).start()
            w_self(a).start()

        @pl.when(away)
        def _():
            w_first_away(a).start()
            w_second_away(a).start()

    def relay_w(a):
        @pl.when(home)
        def _():
            w_first_home(a).wait_recv()
            w_second_home(a).start()

    def pass_first(a):
        w_arrival(a, zh).wait_recv()
        start(w_ring(a, 0))
        start(w_ring(a, 1))

    def pass_second(a):
        w_arrival(a, flip(zh)).wait_recv()
        start(w_ring(a, 2))
        start(w_ring(a, 3))

    def forward_first(a):
        w_ring(a, 0).wait_recv()
        start(w_ring(a, 4))

    def forward_second(a):
        w_ring(a, 3).wait_recv()
        start(w_ring(a, 5))

    def have_w(a):
        def wait():
            for j in (1, 2, 4, 5):
                w_ring(a, j).wait_recv()

        once(("w", a), wait)

    def ring_copy(me, up, down, piece, relay, result, send, recv, j):
        if j == 0:
            src, dst = piece(around(me, 2), 0), relay(0)
        elif j == 1:
            src, dst = piece(around(me, 2), 1), relay(1)
        elif j == 2:
            src, dst = piece(around(me, 1), 1), result(0, 1)
        elif j == 3:
            src, dst = piece(around(me, 3), 0), result(1, 0)
        elif j == 4:
            src, dst = piece(around(me, 1), 0), result(0, 0)
        else:
            src, dst = piece(around(me, 3), 1), result(1, 1)
        return remote(src, dst, send(j), recv(j), down if j % 2 else up)

    def ring_add(me, piece, relay):
        for h, d in ((0, 1), (1, 3)):
            place = piece(around(me, d), h)
            place[...] = (place[...].astype(F32) + relay(h)[...].astype(F32)).astype(BF16)

    def ring_total(me, piece, result, h):
        total = piece(me, h)[...].astype(F32) + result(0, h)[...].astype(F32)
        return total + result(1, h)[...].astype(F32)

    def y_piece(a, s):
        if a == ATTN:
            return lambda q, h: yso.at[q, s, h]
        return lambda q, h: ys.at[a, q, s, h]

    def y_relay(a, s):
        return (lambda h: yao.at[s, h]) if a == ATTN else (lambda h: ya.at[a, s, h])

    def y_result(a, s):
        if a == ATTN:
            return lambda d, h: yro.at[s, d, h]
        return lambda d, h: yr.at[a, s, d, h]

    def y_copy(a, s, j):
        return ring_copy(
            y, y_up, y_down, y_piece(a, s), y_relay(a, s), y_result(a, s),
            lambda i: dy_s.at[a * 2 + s, i], lambda i: dy_r.at[a * 2 + s, i], j,
        )

    def term(a, s):
        have_x(1 if a == ATTN else 0)
        have_g(a)
        part = slice(s * 256, (s + 1) * 256)

        @pl.loop(0, 2)
        def _(k):
            if a == ATTN:
                block = contract_rows(gb[ATTN], xb[1, k, :, part]).astype(BF16)
                for q in range(4):
                    yso[q, s, k] = block[q * 128 : (q + 1) * 128]
            else:
                block = contract_rows(xb[0, k, :, part], gb[a]).astype(BF16)
                for q in range(4):
                    ys[a, q, s, k] = block[:, q * 128 : (q + 1) * 128]

        for j in range(4):
            start(y_copy(a, s, j))

    def combine(a, s):
        y_copy(a, s, 0).wait_recv()
        y_copy(a, s, 1).wait_recv()
        ring_add(y, y_piece(a, s), y_relay(a, s))
        start(y_copy(a, s, 4))
        start(y_copy(a, s, 5))

    def z_place(a, s, slot):
        part = pl.ds(s * 256, 256)
        return zro.at[slot, :, part] if a == ATTN else zr.at[a, slot, part]

    def z_piece(a, s, k):
        return zso.at[s, k] if a == ATTN else zs.at[a, s, k]

    def z_relay(a, s):
        return zwo.at[s] if a == ATTN else zw.at[a, s]

    def z_copy(a, s, i, src, dst, recv, to):
        return remote(src, dst, dz_s.at[a * 2 + s, i], recv, to)

    def z_sem(a, s):
        return dz_r.at[a * 2 + s, zh]

    def z_far_home(a, s):
        return z_copy(a, s, 0, z_piece(a, s, flip(zl1)), z_place(a, s, zh), z_sem(a, s), far)

    def z_far_away(a, s):
        return z_copy(a, s, 0, z_piece(a, s, zl1), z_relay(a, s), zw_r.at[a * 2 + s], far)

    def z_over_home(a, s):
        return z_copy(a, s, 1, z_relay(a, s), z_place(a, s, zh), z_sem(a, s), over_far)

    def z_over_away(a, s):
        return z_copy(a, s, 1, z_piece(a, s, flip(zl1)), z_place(a, s, zh), z_sem(a, s), over_far)

    def z_self(a, s):
        return pltpu.make_async_copy(z_piece(a, s, zl1), z_place(a, s, zh), z_sem(a, s))

    def z_arrival(a, s, slot):
        place = z_place(a, s, slot)
        return remote(place, place, dz_s.at[a * 2 + s, 0], dz_r.at[a * 2 + s, slot], far)

    def sum_y(a, s):
        for j in range(2, 6):
            y_copy(a, s, j).wait_recv()
        for h in (0, 1):
            total = ring_total(y, y_piece(a, s), y_result(a, s), h)
            z_piece(a, s, h)[...] = total.astype(BF16)

        @pl.when(home)
        def _():
            z_far_home(a, s).start()
            z_self(a, s).start()

        @pl.when(away)
        def _():
            z_far_away(a, s).start()
            z_over_away(a, s).start()

    def relay_z(a, s):
        @pl.when(home)
        def _():
            z_far_away(a, s).wait_recv()
            z_over_home(a, s).start()

    def gi_part(s):
        return flip(zl1) if s == 0 else zl1

    def gi_piece(s):
        return lambda b, h: xs.at[gi_part(s), b, h]

    def gi_copy(s, j):
        return ring_copy(
            x, x_up, x_down, gi_piece(s), lambda h: xa.at[s, h], lambda d, h: xr.at[s, d, h],
            lambda i: gx_s.at[s, i], lambda i: gx_r.at[s, i], j,
        )

    def input_term(s):
        for a in (0, 1, 2):
            have_g(a)
            have_w(a)
        k = gi_part(s)

        @pl.loop(0, 4)
        def _(b):
            rows = bank(b)
            total = contract_columns(gb[0, rows], wb[0, k])
            total = total + contract_columns(gb[1, rows], wb[1, k])
            total = total + contract_columns(gb[2, rows], wb[2, k])
            xs[k, b, 0] = total[:128].astype(BF16)
            xs[k, b, 1] = total[128:].astype(BF16)

        for j in range(4):
            start(gi_copy(s, j))

    def gi_combine(s):
        gi_copy(s, 0).wait_recv()
        gi_copy(s, 1).wait_recv()
        ring_add(x, gi_piece(s), lambda h: xa.at[s, h])
        start(gi_copy(s, 4))
        start(gi_copy(s, 5))

    def gi_far():
        return remote(gzs, gz, gg_s, gg_r, far)

    own_out = pltpu.make_async_copy(ownv, gown, loc_sem.at[6])

    def sum_x(s):
        for j in range(2, 6):
            gi_copy(s, j).wait_recv()
        for h in (0, 1):
            total = ring_total(x, gi_piece(s), lambda d, i: xr.at[s, d, i], h)
            rows = slice(h * 128, (h + 1) * 128)
            if s == 0:
                gzs[rows] = total.astype(BF16)
            else:
                ownv[rows] = total
        if s == 0:
            start(gi_far())
        else:
            own_out.start()

    for a in (0, 1, 2, ATTN):
        own_g(a).start()
    for t in (0, 1):
        own_x(t).start()

    barrier = pltpu.get_barrier_semaphore()
    peers = [x_up, x_down, y_up, y_down, side, far, core, over_far]
    for peer in peers:
        pl.semaphore_signal(barrier, inc=1, device_id=peer, device_id_type=MESH)
    pl.semaphore_wait(barrier, len(peers))

    send_far(0)
    send_w(2)
    send_w(0)
    send_w(1)
    relay_w(2)
    pass_first(2)
    send_x(0)
    pass_x(0)
    pass_first(0)
    relay_w(0)
    send_x(1)
    pass_second(2)
    pass_first(1)
    relay_w(1)
    send_g(1)
    send_g(0)
    forward_far(0)
    forward_first(0)
    pass_second(0)
    forward_own(0)
    forward_second(2)
    forward_first(1)
    send_far(1)
    pass_second(1)
    forward_second(0)
    pass_g(1)
    forward_second(1)
    forward_first(2)
    term(1, 0)
    term(1, 1)
    pass_g(0)
    forward_own(1)
    send_g(2)
    combine(1, 0)
    pass_x(1)
    term(0, 0)
    send_g(ATTN)
    term(0, 1)
    pass_g(2)
    combine(1, 1)
    combine(0, 0)
    sum_y(1, 0)
    forward_far(1)
    combine(0, 1)
    term(2, 1)
    pass_g(ATTN)
    term(2, 0)
    sum_y(0, 0)
    sum_y(1, 1)
    sum_y(0, 1)
    combine(2, 1)
    term(ATTN, 0)
    relay_z(1, 0)
    input_term(0)
    combine(2, 0)
    sum_y(2, 1)
    combine(ATTN, 0)
    term(ATTN, 1)
    relay_z(1, 1)
    sum_y(2, 0)
    relay_z(0, 0)
    sum_y(ATTN, 0)
    relay_z(0, 1)
    gi_combine(0)
    combine(ATTN, 1)
    sum_y(ATTN, 1)
    relay_z(2, 0)
    sum_x(0)
    relay_z(2, 1)
    input_term(1)
    relay_z(ATTN, 0)
    relay_z(ATTN, 1)
    gi_combine(1)
    sum_x(1)

    gi_far().wait_recv()
    for a in (0, 1, 2, ATTN):
        for s in (0, 1):
            for slot in (0, 1):
                z_arrival(a, s, slot).wait_recv()
    own_out.wait()
    for copy in sent:
        copy.wait_send()

    @pl.when(home)
    def _():
        for a in (0, 1, 2):
            w_first_home(a).wait_send()
            w_second_home(a).wait_send()
        for a in (0, 1, 2, ATTN):
            for s in (0, 1):
                z_far_home(a, s).wait_send()
                z_over_home(a, s).wait_send()

    @pl.when(away)
    def _():
        for a in (0, 1, 2):
            w_first_away(a).wait_send()
            w_second_away(a).wait_send()
        for a in (0, 1, 2, ATTN):
            for s in (0, 1):
                z_far_away(a, s).wait_send()
                z_over_away(a, s).wait_send()


def finish_kernel(zr_hbm, zro_hbm, gz_hbm, gown_hbm, gi, dq, dk, dv, do, zr, zro, gz, gown, gi_v, dw_v, do_v, sems):
    moves = [(zr_hbm.at[a], zr.at[a]) for a in (0, 1, 2)]
    moves += [(zro_hbm, zro), (gz_hbm, gz), (gown_hbm, gown)]
    loads = [pltpu.make_async_copy(src, dst, sems.at[i]) for i, (src, dst) in enumerate(moves)]
    places = [(dw_v.at[a], out) for a, out in enumerate((dq, dk, dv))]
    places += [(do_v, do), (gi_v, gi)]
    stores = [pltpu.make_async_copy(src, dst, sems.at[6 + i]) for i, (src, dst) in enumerate(places)]
    for copy in loads:
        copy.start()
    for a in (0, 1, 2):
        loads[a].wait()
        dw_v[a] = zr[a, 0].astype(F32) + zr[a, 1].astype(F32)
        stores[a].start()
    loads[3].wait()
    do_v[...] = zro[0].astype(F32) + zro[1].astype(F32)
    stores[3].start()
    loads[4].wait()
    loads[5].wait()
    gi_v[...] = (gown[...] + gz[...].astype(F32)).astype(BF16)
    stores[4].start()
    for copy in stores:
        copy.wait()


def local(inputs, attn_out, grad_out, grad_query, grad_key, grad_value, query_weight, key_weight, value_weight):
    rows, wide, thin = 256, 512, 128
    sem = pltpu.SemaphoreType.DMA
    vm = pltpu.VMEM
    parts = pl.pallas_call(
        exchange_kernel,
        name="exchange",
        out_shape=(
            jax.ShapeDtypeStruct((3, 2, wide, thin), BF16),
            jax.ShapeDtypeStruct((2, thin, wide), BF16),
            jax.ShapeDtypeStruct((rows, wide), BF16),
            jax.ShapeDtypeStruct((rows, wide), F32),
        ),
        in_specs=[pl.BlockSpec(memory_space=pl.ANY)] * 9,
        out_specs=[pl.BlockSpec(memory_space=pl.ANY)] * 4,
        scratch_shapes=[
            vm((2, 2, 4 * rows, wide), BF16),
            vm((4, 4 * rows, wide), BF16),
            vm((3, 2, wide, wide), BF16),
            vm((3, wide, thin), BF16),
            vm((3, 2, rows, thin), BF16),
            vm((2, thin, rows), BF16),
            vm((3, 4, 2, 2, rows, thin), BF16),
            vm((4, 2, 2, thin, rows), BF16),
            vm((3, 2, 2, rows, thin), BF16),
            vm((2, 2, thin, rows), BF16),
            vm((3, 2, 2, 2, rows, thin), BF16),
            vm((2, 2, 2, thin, rows), BF16),
            vm((3, 2, 2, rows, thin), BF16),
            vm((2, 2, thin, rows), BF16),
            vm((2, 4, 2, thin, wide), BF16),
            vm((2, 2, thin, wide), BF16),
            vm((2, 2, 2, thin, wide), BF16),
            vm((rows, wide), BF16),
            vm((rows, wide), F32),
            sem((7,)),
            sem((2,)), sem((2,)),
            sem((2, 6)), sem((2, 6)),
            sem((4,)), sem((4,)),
            sem((4,)), sem((4,)),
            sem((4,)), sem((4,)),
            sem((3, 2)), sem((3, 2)),
            sem((3, 6)), sem((3, 6)),
            sem((8, 6)), sem((8, 6)),
            sem((8, 2)), sem((8, 2)),
            sem((2, 6)), sem((2, 6)),
            sem, sem,
            sem((3,)), sem((8,)),
        ],
        compiler_params=pltpu.CompilerParams(
            collective_id=0, has_side_effects=True, vmem_limit_bytes=56 * 2**20
        ),
    )(
        inputs.reshape(rows, wide),
        grad_out.reshape(rows, wide),
        grad_query.reshape(4 * rows, thin),
        grad_key.reshape(4 * rows, thin),
        grad_value.reshape(4 * rows, thin),
        attn_out.reshape(4 * rows, thin),
        query_weight,
        key_weight,
        value_weight,
    )
    gi, dq, dk, dv, do = pl.pallas_call(
        finish_kernel,
        name="finish",
        out_shape=(
            jax.ShapeDtypeStruct((rows, wide), BF16),
            jax.ShapeDtypeStruct((wide, thin), F32),
            jax.ShapeDtypeStruct((wide, thin), F32),
            jax.ShapeDtypeStruct((wide, thin), F32),
            jax.ShapeDtypeStruct((thin, wide), F32),
        ),
        in_specs=[pl.BlockSpec(memory_space=pl.ANY)] * 4,
        out_specs=[pl.BlockSpec(memory_space=pl.ANY)] * 5,
        scratch_shapes=[
            vm((3, 2, wide, thin), BF16),
            vm((2, thin, wide), BF16),
            vm((rows, wide), BF16),
            vm((rows, wide), F32),
            vm((rows, wide), BF16),
            vm((3, wide, thin), F32),
            vm((thin, wide), F32),
            sem((11,)),
        ],
        compiler_params=pltpu.CompilerParams(vmem_limit_bytes=62 * 2**20),
    )(*parts)
    return gi.reshape(inputs.shape), dq, dk, dv, do


def solution(mesh):
    return jax.shard_map(
        local,
        mesh=mesh,
        in_specs=(
            P("ia", "ja", "ka"),
            P(None, "ja", ("ia", "ka")),
            P("ia", "ja", "ka"),
            P(None, "ja", ("ia", "ka")),
            P(None, "ja", ("ia", "ka")),
            P(None, "ja", ("ia", "ka")),
            P("ka", ("ia", "ja")),
            P("ka", ("ia", "ja")),
            P("ka", ("ia", "ja")),
        ),
        out_specs=(
            P("ia", "ja", "ka"),
            P("ka", ("ia", "ja")),
            P("ka", ("ia", "ja")),
            P("ka", ("ia", "ja")),
            P(("ia", "ja"), "ka"),
        ),
        check_vma=False,
    )
```

```python
import functools

import jax
import jax.numpy as jnp
from jax import lax
from jax.experimental import pallas as pl
from jax.experimental.pallas import tpu as pltpu
from jax.sharding import PartitionSpec as P

MESH = pl.DeviceIdType.MESH
BF16 = jnp.bfloat16
F32 = jnp.float32
ATTN = 3


def contract_rows(a, b):
    return lax.dot_general(a, b, (((0,), (0,)), ((), ())), preferred_element_type=F32)


def contract_columns(a, b):
    return lax.dot_general(a, b, (((1,), (1,)), ((), ())), preferred_element_type=F32)


def exchange_kernel(
    in_ref, go_ref, gq_ref, gk_ref, gv_ref, at_ref, wq_ref, wk_ref, wv_ref,
    zr, zro, gz, gown,
    xb, gb, wb, wr, zw, zwo, ys, yso, ya, yao, yr, yro, zs, zso, xs, xa, xr, gzs, ownv,
    loc_sem, xz_s, xz_r, xo_s, xo_r,
    gz_s, gz_r, gc_s, gc_r, gf_s, gf_r,
    wz_s, wz_r, wy_s, wy_r, dy_s, dy_r, dz_s, dz_r,
    gx_s, gx_r, gg_s, gg_r, wr_r, zw_r,
):
    ia, ja, ka = lax.axis_index("ia"), lax.axis_index("ja"), lax.axis_index("ka")
    x, y, zh = ia, ja % 4, ja // 4
    zl, c = ka // 2, ka % 2
    zl1, zl0 = zl // 2, zl % 2

    def device(x_=None, y_=None, zh_=None, zl_=None, c_=None):
        x_ = x if x_ is None else x_
        y_ = y if y_ is None else y_
        zh_ = zh if zh_ is None else zh_
        zl_ = zl if zl_ is None else zl_
        c_ = c if c_ is None else c_
        return (x_, zh_ * 4 + y_, zl_ * 2 + c_)

    def flip(bit):
        return 1 - bit

    def around(i, d):
        return (i + d) % 4

    zl_side = zl1 * 2 + flip(zl0)
    zl_far = flip(zl1) * 2 + zl0
    side, far, core = device(zl_=zl_side), device(zl_=zl_far), device(c_=flip(c))
    over_far = device(zh_=flip(zh), zl_=zl_far)
    x_up, x_down = device(x_=around(x, 1)), device(x_=around(x, 3))
    y_up, y_down = device(y_=around(y, 1)), device(y_=around(y, 3))

    def remote(src, dst, send, recv, to):
        return pltpu.make_async_remote_copy(
            src_ref=src, dst_ref=dst, send_sem=send, recv_sem=recv,
            device_id=to, device_id_type=MESH,
        )

    sent, seen = [], set()

    def start(copy):
        copy.start()
        sent.append(copy)

    def once(key, wait):
        if key not in seen:
            seen.add(key)
            wait()

    def lanes(k):
        return pl.ds(pl.multiple_of(k * 128, 128), 128)

    def bank(b):
        return pl.ds(pl.multiple_of(b * 256, 256), 256)

    g_refs = (gq_ref, gk_ref, gv_ref, at_ref)
    w_refs = (wq_ref, wk_ref, wv_ref)
    x_refs = (in_ref, go_ref)
    k_own, k_side = zl0 * 2 + c, flip(zl0) * 2 + c

    def own_g(a):
        return pltpu.make_async_copy(g_refs[a], gb.at[a, :, lanes(k_own)], loc_sem.at[a])

    def own_x(t):
        return pltpu.make_async_copy(x_refs[t], xb.at[t, zl1, bank(x)], loc_sem.at[4 + t])

    def g_side(a):
        return remote(g_refs[a], gb.at[a, :, lanes(k_own)], gz_s.at[a], gz_r.at[a], side)

    def g_core(a):
        return remote(g_refs[a], gb.at[a, :, lanes(k_own)], gc_s.at[a], gc_r.at[a], core)

    def g_pass(a):
        place = gb.at[a, :, lanes(k_side)]
        return remote(place, place, gf_s.at[a], gf_r.at[a], core)

    def send_g(a):
        start(g_side(a))
        start(g_core(a))

    def pass_g(a):
        g_side(a).wait_recv()
        start(g_pass(a))

    def have_g(a):
        def wait():
            own_g(a).wait()
            g_core(a).wait_recv()
            g_pass(a).wait_recv()

        once(("g", a), wait)

    def x_far(t):
        return remote(x_refs[t], xb.at[t, zl1, bank(x)], xz_s.at[t], xz_r.at[t], far)

    def x_ring(t, j):
        if j < 2:
            src, dst = x_refs[t], xb.at[t, zl1, bank(x)]
        elif j < 4:
            src = dst = xb.at[t, flip(zl1), bank(x)]
        elif j == 4:
            src = dst = xb.at[t, zl1, bank(around(x, 3))]
        else:
            src = dst = xb.at[t, flip(zl1), bank(around(x, 1))]
        return remote(src, dst, xo_s.at[t, j], xo_r.at[t, j], x_down if j % 2 else x_up)

    def send_far(t):
        start(x_far(t))

    def send_x(t):
        start(x_ring(t, 0))
        start(x_ring(t, 1))

    def pass_x(t):
        x_far(t).wait_recv()
        start(x_ring(t, 2))
        start(x_ring(t, 3))

    def forward_own(t):
        x_ring(t, 0).wait_recv()
        start(x_ring(t, 4))

    def forward_far(t):
        x_ring(t, 3).wait_recv()
        start(x_ring(t, 5))

    def have_x(t):
        def wait():
            own_x(t).wait()
            for j in (1, 2, 4, 5):
                x_ring(t, j).wait_recv()

        once(("x", t), wait)

    home = zl1 == zh
    away = jnp.logical_not(home)

    def w_place(a, k):
        return wb.at[a, k, :, lanes(y)]

    def w_first(a, dst, recv):
        return remote(w_refs[a], dst, wz_s.at[a, 0], recv, over_far)

    def w_first_home(a):
        return w_first(a, wr.at[a], wr_r.at[a])

    def w_first_away(a):
        return w_first(a, w_place(a, zl1), wz_r.at[a, zl1])

    def w_second_home(a):
        return remote(wr.at[a], w_place(a, flip(zl1)), wz_s.at[a, 1], wz_r.at[a, flip(zl1)], far)

    def w_second_away(a):
        return remote(w_refs[a], w_place(a, zl1), wz_s.at[a, 1], wz_r.at[a, zl1], far)

    def w_self(a):
        return pltpu.make_async_copy(w_refs[a], w_place(a, zl1), wz_r.at[a, zl1])

    def w_arrival(a, k):
        return remote(w_place(a, k), w_place(a, k), wz_s.at[a, 0], wz_r.at[a, k], far)

    def w_ring(a, j):
        if j < 2:
            place = wb.at[a, zh, :, lanes(y)]
        elif j < 4:
            place = wb.at[a, flip(zh), :, lanes(y)]
        elif j == 4:
            place = wb.at[a, zh, :, lanes(around(y, 3))]
        else:
            place = wb.at[a, flip(zh), :, lanes(around(y, 1))]
        return remote(place, place, wy_s.at[a, j], wy_r.at[a, j], y_down if j % 2 else y_up)

    def send_w(a):
        @pl.when(home)
        def _():
            w_first_home(a).start()
            w_self(a).start()

        @pl.when(away)
        def _():
            w_first_away(a).start()
            w_second_away(a).start()

    def relay_w(a):
        @pl.when(home)
        def _():
            w_first_home(a).wait_recv()
            w_second_home(a).start()

    def pass_first(a):
        w_arrival(a, zh).wait_recv()
        start(w_ring(a, 0))
        start(w_ring(a, 1))

    def pass_second(a):
        w_arrival(a, flip(zh)).wait_recv()
        start(w_ring(a, 2))
        start(w_ring(a, 3))

    def forward_first(a):
        w_ring(a, 0).wait_recv()
        start(w_ring(a, 4))

    def forward_second(a):
        w_ring(a, 3).wait_recv()
        start(w_ring(a, 5))

    def have_w(a):
        def wait():
            for j in (1, 2, 4, 5):
                w_ring(a, j).wait_recv()

        once(("w", a), wait)

    def ring_copy(me, up, down, piece, relay, result, send, recv, j):
        if j == 0:
            src, dst = piece(around(me, 2), 0), relay(0)
        elif j == 1:
            src, dst = piece(around(me, 2), 1), relay(1)
        elif j == 2:
            src, dst = piece(around(me, 1), 1), result(0, 1)
        elif j == 3:
            src, dst = piece(around(me, 3), 0), result(1, 0)
        elif j == 4:
            src, dst = piece(around(me, 1), 0), result(0, 0)
        else:
            src, dst = piece(around(me, 3), 1), result(1, 1)
        return remote(src, dst, send(j), recv(j), down if j % 2 else up)

    def ring_add(me, piece, relay):
        for h, d in ((0, 1), (1, 3)):
            place = piece(around(me, d), h)
            place[...] = (place[...].astype(F32) + relay(h)[...].astype(F32)).astype(BF16)

    def ring_total(me, piece, result, h):
        total = piece(me, h)[...].astype(F32) + result(0, h)[...].astype(F32)
        return total + result(1, h)[...].astype(F32)

    def y_piece(a, s):
        if a == ATTN:
            return lambda q, h: yso.at[q, s, h]
        return lambda q, h: ys.at[a, q, s, h]

    def y_relay(a, s):
        return (lambda h: yao.at[s, h]) if a == ATTN else (lambda h: ya.at[a, s, h])

    def y_result(a, s):
        if a == ATTN:
            return lambda d, h: yro.at[s, d, h]
        return lambda d, h: yr.at[a, s, d, h]

    def y_copy(a, s, j):
        return ring_copy(
            y, y_up, y_down, y_piece(a, s), y_relay(a, s), y_result(a, s),
            lambda i: dy_s.at[a * 2 + s, i], lambda i: dy_r.at[a * 2 + s, i], j,
        )

    def term(a, s):
        have_x(1 if a == ATTN else 0)
        have_g(a)
        part = slice(s * 256, (s + 1) * 256)

        @pl.loop(0, 2)
        def _(k):
            if a == ATTN:
                block = contract_rows(gb[ATTN], xb[1, k, :, part]).astype(BF16)
                for q in range(4):
                    yso[q, s, k] = block[q * 128 : (q + 1) * 128]
            else:
                block = contract_rows(xb[0, k, :, part], gb[a]).astype(BF16)
                for q in range(4):
                    ys[a, q, s, k] = block[:, q * 128 : (q + 1) * 128]

        for j in range(4):
            start(y_copy(a, s, j))

    def combine(a, s):
        y_copy(a, s, 0).wait_recv()
        y_copy(a, s, 1).wait_recv()
        ring_add(y, y_piece(a, s), y_relay(a, s))
        start(y_copy(a, s, 4))
        start(y_copy(a, s, 5))

    def z_place(a, s, slot):
        part = pl.ds(s * 256, 256)
        return zro.at[slot, :, part] if a == ATTN else zr.at[a, slot, part]

    def z_piece(a, s, k):
        return zso.at[s, k] if a == ATTN else zs.at[a, s, k]

    def z_relay(a, s):
        return zwo.at[s] if a == ATTN else zw.at[a, s]

    def z_copy(a, s, i, src, dst, recv, to):
        return remote(src, dst, dz_s.at[a * 2 + s, i], recv, to)

    def z_sem(a, s):
        return dz_r.at[a * 2 + s, zh]

    def z_far_home(a, s):
        return z_copy(a, s, 0, z_piece(a, s, flip(zl1)), z_place(a, s, zh), z_sem(a, s), far)

    def z_far_away(a, s):
        return z_copy(a, s, 0, z_piece(a, s, zl1), z_relay(a, s), zw_r.at[a * 2 + s], far)

    def z_over_home(a, s):
        return z_copy(a, s, 1, z_relay(a, s), z_place(a, s, zh), z_sem(a, s), over_far)

    def z_over_away(a, s):
        return z_copy(a, s, 1, z_piece(a, s, flip(zl1)), z_place(a, s, zh), z_sem(a, s), over_far)

    def z_self(a, s):
        return pltpu.make_async_copy(z_piece(a, s, zl1), z_place(a, s, zh), z_sem(a, s))

    def z_arrival(a, s, slot):
        place = z_place(a, s, slot)
        return remote(place, place, dz_s.at[a * 2 + s, 0], dz_r.at[a * 2 + s, slot], far)

    def sum_y(a, s):
        for j in range(2, 6):
            y_copy(a, s, j).wait_recv()
        for h in (0, 1):
            total = ring_total(y, y_piece(a, s), y_result(a, s), h)
            z_piece(a, s, h)[...] = total.astype(BF16)

        @pl.when(home)
        def _():
            z_far_home(a, s).start()
            z_self(a, s).start()

        @pl.when(away)
        def _():
            z_far_away(a, s).start()
            z_over_away(a, s).start()

    def relay_z(a, s):
        @pl.when(home)
        def _():
            z_far_away(a, s).wait_recv()
            z_over_home(a, s).start()

    def gi_part(s):
        return flip(zl1) if s == 0 else zl1

    def gi_piece(s):
        return lambda b, h: xs.at[gi_part(s), b, h]

    def gi_copy(s, j):
        return ring_copy(
            x, x_up, x_down, gi_piece(s), lambda h: xa.at[s, h], lambda d, h: xr.at[s, d, h],
            lambda i: gx_s.at[s, i], lambda i: gx_r.at[s, i], j,
        )

    def input_term(s):
        for a in (0, 1, 2):
            have_g(a)
            have_w(a)
        k = gi_part(s)

        @pl.loop(0, 4)
        def _(b):
            rows = bank(b)
            total = contract_columns(gb[0, rows], wb[0, k])
            total = total + contract_columns(gb[1, rows], wb[1, k])
            total = total + contract_columns(gb[2, rows], wb[2, k])
            xs[k, b, 0] = total[:128].astype(BF16)
            xs[k, b, 1] = total[128:].astype(BF16)

        for j in range(4):
            start(gi_copy(s, j))

    def gi_combine(s):
        gi_copy(s, 0).wait_recv()
        gi_copy(s, 1).wait_recv()
        ring_add(x, gi_piece(s), lambda h: xa.at[s, h])
        start(gi_copy(s, 4))
        start(gi_copy(s, 5))

    def gi_far():
        return remote(gzs, gz, gg_s, gg_r, far)

    own_out = pltpu.make_async_copy(ownv, gown, loc_sem.at[6])

    def sum_x(s):
        for j in range(2, 6):
            gi_copy(s, j).wait_recv()
        for h in (0, 1):
            total = ring_total(x, gi_piece(s), lambda d, i: xr.at[s, d, i], h)
            rows = slice(h * 128, (h + 1) * 128)
            if s == 0:
                gzs[rows] = total.astype(BF16)
            else:
                ownv[rows] = total
        if s == 0:
            start(gi_far())
        else:
            own_out.start()

    for a in (0, 1, 2, ATTN):
        own_g(a).start()
    for t in (0, 1):
        own_x(t).start()

    barrier = pltpu.get_barrier_semaphore()
    peers = [x_up, x_down, y_up, y_down, side, far, core, over_far]
    for peer in peers:
        pl.semaphore_signal(barrier, inc=1, device_id=peer, device_id_type=MESH)
    pl.semaphore_wait(barrier, len(peers))

    send_far(0)
    send_w(0)
    send_x(0)
    send_w(1)
    send_w(2)
    pass_first(0)
    relay_w(0)
    relay_w(1)
    forward_first(0)
    pass_first(1)
    pass_x(0)
    relay_w(2)
    send_g(2)
    pass_second(0)
    pass_first(2)
    send_g(1)
    send_x(1)
    forward_second(0)
    send_far(1)
    forward_own(0)
    pass_second(1)
    forward_first(1)
    forward_far(0)
    pass_second(2)
    forward_first(2)
    send_g(0)
    send_g(ATTN)
    forward_second(1)
    pass_g(2)
    forward_second(2)
    term(2, 0)
    pass_g(1)
    forward_own(1)
    term(2, 1)
    term(1, 1)
    pass_x(1)
    combine(2, 0)
    term(1, 0)
    pass_g(0)
    combine(2, 1)
    combine(1, 1)
    sum_y(2, 0)
    combine(1, 0)
    forward_far(1)
    term(0, 0)
    term(0, 1)
    sum_y(1, 1)
    sum_y(2, 1)
    pass_g(ATTN)
    input_term(0)
    combine(0, 0)
    term(ATTN, 0)
    sum_y(1, 0)
    combine(0, 1)
    input_term(1)
    relay_z(2, 1)
    combine(ATTN, 0)
    sum_y(0, 0)
    term(ATTN, 1)
    gi_combine(0)
    relay_z(2, 0)
    sum_y(0, 1)
    relay_z(1, 1)
    relay_z(1, 0)
    sum_y(ATTN, 0)
    combine(ATTN, 1)
    sum_y(ATTN, 1)
    relay_z(0, 0)
    gi_combine(1)
    relay_z(0, 1)
    sum_x(0)
    relay_z(ATTN, 1)
    sum_x(1)
    relay_z(ATTN, 0)

    gi_far().wait_recv()
    for a in (0, 1, 2, ATTN):
        for s in (0, 1):
            for slot in (0, 1):
                z_arrival(a, s, slot).wait_recv()
    own_out.wait()
    for copy in sent:
        copy.wait_send()

    @pl.when(home)
    def _():
        for a in (0, 1, 2):
            w_first_home(a).wait_send()
            w_second_home(a).wait_send()
        for a in (0, 1, 2, ATTN):
            for s in (0, 1):
                z_far_home(a, s).wait_send()
                z_over_home(a, s).wait_send()

    @pl.when(away)
    def _():
        for a in (0, 1, 2):
            w_first_away(a).wait_send()
            w_second_away(a).wait_send()
        for a in (0, 1, 2, ATTN):
            for s in (0, 1):
                z_far_away(a, s).wait_send()
                z_over_away(a, s).wait_send()


def finish_kernel(zr_hbm, zro_hbm, gz_hbm, gown_hbm, gi, dq, dk, dv, do, zr, zro, gz, gown, gi_v, dw_v, do_v, sems):
    moves = [(zr_hbm.at[a], zr.at[a]) for a in (0, 1, 2)]
    moves += [(zro_hbm, zro), (gz_hbm, gz), (gown_hbm, gown)]
    loads = [pltpu.make_async_copy(src, dst, sems.at[i]) for i, (src, dst) in enumerate(moves)]
    places = [(dw_v.at[a], out) for a, out in enumerate((dq, dk, dv))]
    places += [(do_v, do), (gi_v, gi)]
    stores = [pltpu.make_async_copy(src, dst, sems.at[6 + i]) for i, (src, dst) in enumerate(places)]
    for copy in loads:
        copy.start()
    for a in (0, 1, 2):
        loads[a].wait()
        dw_v[a] = zr[a, 0].astype(F32) + zr[a, 1].astype(F32)
        stores[a].start()
    loads[3].wait()
    do_v[...] = zro[0].astype(F32) + zro[1].astype(F32)
    stores[3].start()
    loads[4].wait()
    loads[5].wait()
    gi_v[...] = (gown[...] + gz[...].astype(F32)).astype(BF16)
    stores[4].start()
    for copy in stores:
        copy.wait()


def local(inputs, attn_out, grad_out, grad_query, grad_key, grad_value, query_weight, key_weight, value_weight):
    rows, wide, thin = 256, 512, 128
    sem = pltpu.SemaphoreType.DMA
    vm = pltpu.VMEM
    parts = pl.pallas_call(
        exchange_kernel,
        name="exchange",
        out_shape=(
            jax.ShapeDtypeStruct((3, 2, wide, thin), BF16),
            jax.ShapeDtypeStruct((2, thin, wide), BF16),
            jax.ShapeDtypeStruct((rows, wide), BF16),
            jax.ShapeDtypeStruct((rows, wide), F32),
        ),
        in_specs=[pl.BlockSpec(memory_space=pl.ANY)] * 9,
        out_specs=[pl.BlockSpec(memory_space=pl.ANY)] * 4,
        scratch_shapes=[
            vm((2, 2, 4 * rows, wide), BF16),
            vm((4, 4 * rows, wide), BF16),
            vm((3, 2, wide, wide), BF16),
            vm((3, wide, thin), BF16),
            vm((3, 2, rows, thin), BF16),
            vm((2, thin, rows), BF16),
            vm((3, 4, 2, 2, rows, thin), BF16),
            vm((4, 2, 2, thin, rows), BF16),
            vm((3, 2, 2, rows, thin), BF16),
            vm((2, 2, thin, rows), BF16),
            vm((3, 2, 2, 2, rows, thin), BF16),
            vm((2, 2, 2, thin, rows), BF16),
            vm((3, 2, 2, rows, thin), BF16),
            vm((2, 2, thin, rows), BF16),
            vm((2, 4, 2, thin, wide), BF16),
            vm((2, 2, thin, wide), BF16),
            vm((2, 2, 2, thin, wide), BF16),
            vm((rows, wide), BF16),
            vm((rows, wide), F32),
            sem((7,)),
            sem((2,)), sem((2,)),
            sem((2, 6)), sem((2, 6)),
            sem((4,)), sem((4,)),
            sem((4,)), sem((4,)),
            sem((4,)), sem((4,)),
            sem((3, 2)), sem((3, 2)),
            sem((3, 6)), sem((3, 6)),
            sem((8, 6)), sem((8, 6)),
            sem((8, 2)), sem((8, 2)),
            sem((2, 6)), sem((2, 6)),
            sem, sem,
            sem((3,)), sem((8,)),
        ],
        compiler_params=pltpu.CompilerParams(
            collective_id=0, has_side_effects=True, vmem_limit_bytes=56 * 2**20
        ),
    )(
        inputs.reshape(rows, wide),
        grad_out.reshape(rows, wide),
        grad_query.reshape(4 * rows, thin),
        grad_key.reshape(4 * rows, thin),
        grad_value.reshape(4 * rows, thin),
        attn_out.reshape(4 * rows, thin),
        query_weight,
        key_weight,
        value_weight,
    )
    gi, dq, dk, dv, do = pl.pallas_call(
        finish_kernel,
        name="finish",
        out_shape=(
            jax.ShapeDtypeStruct((rows, wide), BF16),
            jax.ShapeDtypeStruct((wide, thin), F32),
            jax.ShapeDtypeStruct((wide, thin), F32),
            jax.ShapeDtypeStruct((wide, thin), F32),
            jax.ShapeDtypeStruct((thin, wide), F32),
        ),
        in_specs=[pl.BlockSpec(memory_space=pl.ANY)] * 4,
        out_specs=[pl.BlockSpec(memory_space=pl.ANY)] * 5,
        scratch_shapes=[
            vm((3, 2, wide, thin), BF16),
            vm((2, thin, wide), BF16),
            vm((rows, wide), BF16),
            vm((rows, wide), F32),
            vm((rows, wide), BF16),
            vm((3, wide, thin), F32),
            vm((thin, wide), F32),
            sem((11,)),
        ],
        compiler_params=pltpu.CompilerParams(vmem_limit_bytes=62 * 2**20),
    )(*parts)
    return gi.reshape(inputs.shape), dq, dk, dv, do


def solution(mesh):
    return jax.shard_map(
        local,
        mesh=mesh,
        in_specs=(
            P("ia", "ja", "ka"),
            P(None, "ja", ("ia", "ka")),
            P("ia", "ja", "ka"),
            P(None, "ja", ("ia", "ka")),
            P(None, "ja", ("ia", "ka")),
            P(None, "ja", ("ia", "ka")),
            P("ka", ("ia", "ja")),
            P("ka", ("ia", "ja")),
            P("ka", ("ia", "ja")),
        ),
        out_specs=(
            P("ia", "ja", "ka"),
            P("ka", ("ia", "ja")),
            P("ka", ("ia", "ja")),
            P("ka", ("ia", "ja")),
            P(("ia", "ja"), "ka"),
        ),
        check_vma=False,
    )
```
